256 devices in a mesh: ctx: 4 (over z_lo), zero: 64 (over z_hi, x, y, core).
Axes of the slice: x: 4, y: 4, z: 8 (z_hi: 2, z_lo: 4; z = z_hi * 4 + z_lo), core: 2. Of those that a mesh axis runs over, the one named last changes fastest.
Arguments:
- proj: bfloat16 [64, 512, 3, 4096], P('zero', 'ctx'), may hold values from -6 to 6
- short_weight: float32 [3, 3, 4096], P(None, None, ('ctx', 'zero')), may hold values from -3 to 3
- residue: float32 [16, 4096], P(None, ('ctx', 'zero')), may hold values from -0.125 to 0.125
- log_decay: float32 [16, 4096], P(None, ('ctx', 'zero')), as said below
- cotangent: bfloat16 [64, 512, 4096], P('zero', 'ctx'), may hold values from -6 to 6
Outputs:
- output: bfloat16 [64, 512, 4096], P('zero', 'ctx')
- proj_grad: bfloat16 [64, 512, 3, 4096], P('zero', 'ctx')
- tap_grad: float32 [3, 3, 4096], P(None, None, ('ctx', 'zero'))
- residue_grad: float32 [16, 4096], P(None, ('ctx', 'zero'))
- decay_grad: float32 [16, 4096], P(None, ('ctx', 'zero'))
The draws below stay inside these ranges and needn't reach their ends.
Inputs may be any that keep to these rules, and one draw needn't show every extreme that they name: exp(log_decay) lies between 0.3 / 512 and max(1 / 30, 2 / 512).
All inputs are finite; a program needn't handle non-finite values.
Results may differ from the reference program's by a relative error of at most 0.0058.
Values may be sent and summed in bfloat16 or wider, within the bound.
No kernel may reach another device: no remote copies, remote signals or barrier semaphores. Data moves between devices by JAX's collectives and lax.ppermute only.
A program may use at most 256 MiB of HBM per device.

```python
import math
import jax
import jax.numpy as jnp
from jax import lax

CH = 4096
ORDER = 16
SHORT = 3
SEQ = 512
BATCH = 64


def draw_log_decay(key, part):
    key = jax.random.fold_in(key, 11)
    lowest = math.log(0.3 / SEQ)
    highest = math.log(1.0 / 30.0)
    result = jax.random.uniform(jax.random.fold_in(key, 2), (ORDER, CH), minval=lowest, maxval=highest)
    return result.astype(jnp.float32)


def shard_levels(rng, dims, shards, low, top_value):
    loudness, own = 1.0, jax.random.fold_in(rng, 6)
    for dim, blocks in shards:
        steps = jnp.exp(jax.random.uniform(jax.random.fold_in(own, dim), (blocks,), jnp.float32, low / len(shards), top_value / len(shards)))
        loudness = loudness * jnp.repeat(steps, dims[dim] // blocks).reshape([-1 if axis == dim else 1 for axis in range(len(dims))])
    return loudness


def centred(own_key, dims, width, limit, split=(), kind=jnp.bfloat16):
    drawn = width * jax.random.normal(own_key, dims, jnp.float32)
    if split:
        drawn = drawn * shard_levels(own_key, dims, split, -0.22, 0.18)
    return jnp.clip(drawn, -limit, limit).astype(kind)


def setup_inputs(seed: int = 0) -> dict:
    key_list = jax.random.split(jax.random.key(seed), 6)
    return {
        "proj": centred(key_list[0], (BATCH, SEQ, 3, CH), 1.0, 6.0, ((0, 64), (1, 4))),
        "short_weight": centred(key_list[1], (3, SHORT, CH), 0.6, 3.0, ((2, 256),), jnp.float32),
        "residue": centred(key_list[2], (ORDER, CH), (ORDER * SEQ // 4) ** -0.5, 0.125, ((1, 256),), jnp.float32),
        "log_decay": draw_log_decay(jax.random.fold_in(key_list[5], 71), 0),
        "cotangent": centred(key_list[4], (BATCH, SEQ, CH), 1.0, 6.0, ((0, 64), (1, 4))),
    }


def rounded(values_in):
    return lax.optimization_barrier(values_in.astype(jnp.bfloat16)).astype(jnp.float32)

def taps_forward(signal, weights):
    positions = signal.shape[0]
    summed = jnp.zeros(signal.shape, jnp.float32)
    for offset in range(SHORT):
        shifted = jnp.pad(signal, ((offset, 0), (0, 0), (0, 0)))[:positions]
        summed = summed + weights[:, offset, :] * shifted
    return summed

def taps_backward(grads, weights):
    summed = jnp.zeros(grads.shape, jnp.float32)
    for offset in range(SHORT):
        shifted = jnp.pad(grads, ((0, offset), (0, 0), (0, 0)))[offset:]
        summed = summed + weights[:, offset, :] * shifted
    return summed

def taps_weight_grad(grads, signal):
    positions = signal.shape[0]
    columns = []
    for offset in range(SHORT):
        shifted = jnp.pad(signal, ((offset, 0), (0, 0), (0, 0)))[:positions]
        columns.append(lax.optimization_barrier(jnp.sum(grads * shifted, axis=0)))
    return jnp.stack(columns, axis=1)

def modal_filter(residue, log_decay):
    decay_rate = jnp.exp(log_decay)
    positions = jnp.arange(SEQ).astype(log_decay.dtype)
    decay = jnp.exp(-decay_rate[:, None, :] * positions[None, :, None])
    return (lax.optimization_barrier(jnp.sum(residue[:, None, :] * decay, axis=0)), decay, decay_rate, positions)

def reference(proj, short_weight, residue, log_decay, cotangent):
    kernel, decay, decay_rate, positions = modal_filter(residue, log_decay)
    padded_len = 2 * SEQ
    spectrum = jnp.fft.rfft(kernel, n=padded_len, axis=0)

    def sequence_step(totals, inputs):
        kernel_sum, tap_sum = totals
        signal, upstream = inputs
        signal = signal.astype(jnp.float32)
        upstream = upstream.astype(jnp.float32)
        filtered = taps_forward(signal, short_weight)
        queries = filtered[:, 0]
        keys_part = filtered[:, 1]
        values = filtered[:, 2]
        gated = rounded(keys_part * values)
        gated_hat = jnp.fft.rfft(gated, n=padded_len, axis=0)
        convolved = rounded(jnp.fft.irfft(gated_hat * spectrum, n=padded_len, axis=0)[:SEQ])
        output = (queries * convolved).astype(jnp.bfloat16)
        gate_grad = rounded(upstream * queries)
        grad_hat = jnp.fft.rfft(gate_grad, n=padded_len, axis=0)
        gated_grad = rounded(jnp.fft.irfft(jnp.conj(spectrum) * grad_hat, n=padded_len, axis=0)[:SEQ])
        kernel_grad = jnp.fft.irfft(grad_hat * jnp.conj(gated_hat), n=padded_len, axis=0)[:SEQ]
        filtered_grad = jnp.stack([upstream * convolved, gated_grad * values, gated_grad * keys_part], axis=1)
        proj_grad = taps_backward(filtered_grad, short_weight).astype(jnp.bfloat16)
        tap_part = taps_weight_grad(filtered_grad, signal)
        return ((kernel_sum + kernel_grad, tap_sum + tap_part), (output, proj_grad))
    initial = (jnp.zeros((SEQ, CH), jnp.float32), jnp.zeros((3, SHORT, CH), jnp.float32))
    (kernel_sum, tap_sum), (outputs, proj_grads) = lax.scan(sequence_step, initial, (proj, cotangent))
    factor = 1.0 / SEQ
    weighted = (kernel_sum * factor)[None] * decay
    residue_grad = lax.optimization_barrier(jnp.sum(weighted, axis=1))
    decay_grad = -lax.optimization_barrier(jnp.sum(weighted * positions[None, :, None], axis=1)) * residue * decay_rate
    return (outputs, proj_grads, tap_sum * factor, residue_grad, decay_grad)
```

```python
import functools

import jax
import jax.numpy as jnp
import ml_dtypes
import numpy as np
from jax import lax
from jax.experimental import pallas as pl
from jax.experimental.pallas import tpu as pltpu
from jax.sharding import PartitionSpec as P

SHORT = 3
ORDER = 16
GROUP = 4
LANES = 128
BF = jnp.bfloat16
F32 = jnp.float32


def split_table(table):
    high = table.astype(ml_dtypes.bfloat16)
    low = (table - high.astype(np.float64)).astype(ml_dtypes.bfloat16)
    return high, low


def tables(chunk):
    padded = 2 * chunk
    index = np.arange(chunk)
    angle = 2.0 * np.pi / padded * (np.outer(index, index) % padded)
    parity = np.where(index % 2 == 0, 1.0, -1.0)
    cosine, sine = np.cos(angle), np.sin(angle)
    sine[0] = parity
    forward = np.concatenate([cosine, sine], 0)
    weight = np.where(index == 0, 1.0, 2.0) / padded
    backward = np.concatenate([cosine * weight[:, None], sine * weight[:, None]], 0).T
    fwd_hi, fwd_lo = split_table(forward)
    inv_hi, inv_lo = split_table(backward)
    fwd2 = np.concatenate([fwd_hi, fwd_lo], 1)
    reverse = np.eye(chunk)[::-1].astype(ml_dtypes.bfloat16)
    rev2 = np.concatenate([reverse, reverse], 1)
    sums = np.kron(np.eye(ORDER), np.ones((1, 8))).astype(np.float32)
    ramp = np.kron(np.eye(ORDER), np.arange(8.0)[None]).astype(np.float32)
    return fwd2, inv_hi, inv_lo, rev2, sums, ramp


def mxu(left, right):
    return jnp.dot(left, right, preferred_element_type=F32)


def exact_dot(left, right):
    return jnp.dot(left, right, preferred_element_type=F32, precision=lax.Precision.HIGHEST)


def halves(values):
    high = values.astype(BF)
    return high, (values - high.astype(F32)).astype(BF)


def down(values, above, offset):
    if offset == 0:
        return values
    rows = values.shape[0]
    return jnp.concatenate([above, values], 0)[8 - offset : 8 - offset + rows]


def up(values, below, offset):
    if offset == 0:
        return values
    rows = values.shape[0]
    return jnp.concatenate([values, below], 0)[offset : offset + rows]


def taps(values, above, weights, which):
    total = weights[3 * which][None] * values
    for offset in range(1, SHORT):
        total = total + weights[3 * which + offset][None] * down(values, above, offset)
    return total


def first_powers(rate):
    steps = lax.broadcasted_iota(jnp.int32, (8, LANES), 0).astype(F32)
    rates = jnp.broadcast_to(rate, (8, LANES))
    return jnp.exp(-rates * steps), jnp.exp(-8.0 * rates)


def moments(par_ref, sources, accs, lanes, tiles):
    for group in range(0, ORDER, GROUP):
        modes = range(group, group + GROUP)
        rates = [jnp.exp(par_ref[ORDER + m : ORDER + m + 1, lanes]) for m in modes]
        powers, steps = map(list, zip(*[first_powers(r) for r in rates]))
        plain = [[None] * GROUP for _ in sources]
        summed = [[None] * GROUP for _ in sources]
        for tile in range(tiles):
            rows = slice(8 * tile, 8 * tile + 8)
            values = [s[rows, lanes] for s in sources]
            for g in range(GROUP):
                for s, value in enumerate(values):
                    term = powers[g] * value
                    if tile == 0:
                        plain[s][g] = term
                        summed[s][g] = term
                    else:
                        plain[s][g] = plain[s][g] + term
                        if tile < tiles - 1:
                            summed[s][g] = summed[s][g] + plain[s][g]
                if tile < tiles - 1:
                    powers[g] = powers[g] * steps[g]
        for s in range(len(sources)):
            for g, m in enumerate(modes):
                accs[2 * s][8 * m : 8 * m + 8, lanes] = plain[s][g]
                accs[2 * s + 1][8 * m : 8 * m + 8, lanes] = summed[s][g]


def finish(sums, ramp, plain, summed, tiles):
    zeroth = exact_dot(sums, plain)
    first = 8.0 * ((tiles - 1.0) * zeroth - exact_dot(sums, summed)) + exact_dot(ramp, plain)
    return zeroth, first


def state_kernel(
    proj, above, cot, par, rev2, sums, ramp, gated_out, grad_out, state_out, send_out, xrev, grads, *accs
):
    chunk, block = cot.shape
    tiles = chunk // 8
    weights = [par[2 * ORDER + i] for i in range(9)]
    filtered = [
        taps(proj[i].astype(F32), above[i].astype(F32), weights, i) for i in range(3)
    ]
    gated = (filtered[1] * filtered[2]).astype(BF)
    gate_grad = (cot[...].astype(F32) * filtered[0]).astype(BF)
    gated_out[...] = gated
    grad_out[...] = gate_grad
    grads[...] = gate_grad.astype(F32)
    xrev[...] = mxu(rev2[:, :chunk], gated)

    @pl.loop(0, block // LANES)
    def _(step):
        lanes = pl.ds(pl.multiple_of(step * LANES, LANES), LANES)
        moments(par, [xrev, grads], accs, lanes, tiles)

    s0, s1 = finish(sums[...], ramp[...], accs[0][...], accs[1][...], tiles)
    p0, p1 = finish(sums[...], ramp[...], accs[2][...], accs[3][...], tiles)
    state_out[0:16] = s0
    state_out[16:32] = s1
    state_out[32:48] = p0
    state_out[48:64] = p1
    send_out[0] = s0.astype(BF)
    send_out[1] = p0.astype(BF)


def local_kernel(
    gated, grad, par, fwd2, inv_hi, inv_lo, sums, ramp, conv_out, back_out, modal_out, kern, corr, *accs
):
    chunk, block = gated.shape
    tiles = chunk // 8

    @pl.loop(0, block // LANES)
    def _(step):
        lanes = pl.ds(pl.multiple_of(step * LANES, LANES), LANES)
        half = ORDER // 2
        for group in (0, half):
            modes = range(group, group + half)
            rates = [jnp.exp(par[ORDER + m : ORDER + m + 1, lanes]) for m in modes]
            powers, steps = map(list, zip(*[first_powers(r) for r in rates]))
            gains = [jnp.broadcast_to(par[m : m + 1, lanes], (8, LANES)) for m in modes]
            powers = [p * g for p, g in zip(powers, gains)]
            for tile in range(tiles):
                rows = slice(8 * tile, 8 * tile + 8)
                parts = list(powers)
                while len(parts) > 1:
                    parts = [a + b for a, b in zip(parts[::2], parts[1::2])]
                total = parts[0]
                if group:
                    total = total + kern[rows, lanes]
                kern[rows, lanes] = total
                powers = [p * s for p, s in zip(powers, steps)]

    def transform(values):
        return mxu(fwd2[...], jnp.concatenate([values, values], 0))

    def inverse(values):
        high, low = halves(values)
        return mxu(inv_hi[...], high) + mxu(inv_hi[...], low) + mxu(inv_lo[...], high)

    x, g = transform(gated[...]), transform(grad[...])
    k_hi, k_lo = halves(kern[...])
    k = transform(k_hi) + mxu(fwd2[:, :chunk], k_lo)
    first = lax.broadcasted_iota(jnp.int32, (chunk, block), 0) == 0

    def product(a, b, sign):
        a_re, a_im, b_re, b_im = a[:chunk], a[chunk:], b[:chunk], b[chunk:]
        both = a_im * b_im
        real = a_re * b_re + jnp.where(first, 0.0, -sign * both)
        imag = jnp.where(first, both, a_re * b_im + sign * (a_im * b_re))
        return jnp.concatenate([real, imag], 0)

    conv_out[...] = inverse(product(k, x, 1.0))
    back_out[...] = inverse(product(k, g, -1.0))
    corr[...] = inverse(product(x, g, -1.0))

    @pl.loop(0, block // LANES)
    def _(step):
        lanes = pl.ds(pl.multiple_of(step * LANES, LANES), LANES)
        moments(par, [corr], accs, lanes, tiles)

    m0, m1 = finish(sums[...], ramp[...], accs[0][...], accs[1][...], tiles)
    modal_out[0:16] = m0
    modal_out[16:32] = m1


def final_kernel(
    proj, above, below, cot, cot_below, par, state, before, after, modal, conv, back, rev2,
    out, proj_grad, grads, conv_x, back_x,
):
    chunk, block = cot.shape
    tiles = chunk // 8
    residue = par[0:ORDER]
    rate = jnp.exp(par[ORDER : 2 * ORDER])
    one = jnp.exp(-rate)
    whole = jnp.exp(-float(chunk) * rate)
    entering = before[0].astype(F32) + whole * (before[1].astype(F32) + whole * before[2].astype(F32))
    leaving = after[0].astype(F32) + whole * (after[1].astype(F32) + whole * after[2].astype(F32))
    s0, s1, p0, p1 = (state[16 * i : 16 * i + 16] for i in range(4))
    grads[0:16] = modal[0:16] + one * p0 * entering
    grads[16:32] = modal[16:32] + one * (
        p1 * entering + s1 * leaving + p0 * entering + chunk * whole * entering * leaving
    )
    in_gain = one * residue * entering
    out_gain = one * residue * leaving
    half = ORDER // 2
    for step in range(block // LANES):
        lanes = slice(step * LANES, step * LANES + LANES)
        for group in (0, half):
            modes = range(group, group + half)
            made = [first_powers(rate[m : m + 1, lanes]) for m in modes]
            powers, steps = map(list, zip(*made))
            gain_x = [jnp.broadcast_to(in_gain[m : m + 1, lanes], (8, LANES)) for m in modes]
            gain_g = [jnp.broadcast_to(out_gain[m : m + 1, lanes], (8, LANES)) for m in modes]
            for tile in range(tiles):
                rows = slice(8 * tile, 8 * tile + 8)
                sum_x = conv[rows, lanes] if group == 0 else conv_x[rows, lanes]
                sum_g = None if group == 0 else back_x[rows, lanes]
                for p, gx, gg in zip(powers, gain_x, gain_g):
                    sum_x = sum_x + gx * p
                    sum_g = gg * p if sum_g is None else sum_g + gg * p
                conv_x[rows, lanes] = sum_x
                back_x[rows, lanes] = sum_g
                if tile < tiles - 1:
                    powers = [p * s for p, s in zip(powers, steps)]

    weights = [par[2 * ORDER + i] for i in range(9)]
    signal = [proj[i].astype(F32) for i in range(3)]
    halo = [above[i].astype(F32) for i in range(3)]
    upstream = cot[...].astype(F32)
    queries, keys, values = (taps(signal[i], halo[i], weights, i) for i in range(3))
    convolved = conv_x[...].astype(BF).astype(F32)
    b_hi, b_lo = halves(back_x[...])
    crossed = mxu(rev2[...], jnp.concatenate([b_hi, b_lo], 0))
    gated_grad = (back[...] + crossed).astype(BF).astype(F32)
    out[...] = (queries * convolved).astype(BF)
    fgrad = [upstream * convolved, gated_grad * values, gated_grad * keys]

    tails = [below[i].astype(F32) for i in range(3)]
    q_r, k_r, v_r = (taps(tails[i], signal[i][chunk - 8 :], weights, i) for i in range(3))
    cot_r = cot_below[...].astype(F32)
    x_r = (k_r * v_r).astype(BF).astype(F32)
    g_r = (cot_r * q_r).astype(BF).astype(F32)
    h0 = one * (whole * entering + s0) + x_r[0:1]
    h1 = one * h0 + x_r[1:2]
    e1 = (leaving - g_r[0:1]) / one
    rows8 = lax.broadcasted_iota(jnp.int32, (8, block), 0)

    def two_rows(a, b):
        a = jnp.sum(residue * a, axis=0, keepdims=True)
        b = jnp.sum(residue * b, axis=0, keepdims=True)
        both = jnp.where(rows8 == 0, a, jnp.where(rows8 == 1, b, 0.0))
        return both.astype(BF).astype(F32)

    conv_r, back_r = two_rows(h0, h1), two_rows(leaving, e1)
    fgrad_r = [cot_r * conv_r, back_r * v_r, back_r * k_r]

    lines = []
    for i in range(3):
        total = weights[3 * i][None] * fgrad[i]
        for offset in range(1, SHORT):
            total = total + weights[3 * i + offset][None] * up(fgrad[i], fgrad_r[i], offset)
        proj_grad[i] = total.astype(BF)
        for offset in range(SHORT):
            moved = down(signal[i], halo[i], offset)
            lines.append(jnp.sum(fgrad[i] * moved, axis=0, keepdims=True))
    for i in range(9):
        grads[2 * ORDER + i : 2 * ORDER + i + 1] = lines[i]


def body(names, proj, short_weight, residue, log_decay, cotangent):
    ctx, devices, n_ctx = names
    chunk, channels = cotangent.shape[1:]
    own = residue.shape[1]
    seq = chunk * n_ctx
    n_dev = channels // own
    rows = 2 * ORDER + 9
    block = 512 if channels % 512 == 0 else channels
    grid = (channels // block,)
    fwd2, inv_hi, inv_lo, rev2, sums, ramp = (jnp.asarray(t) for t in tables(chunk))

    packed = jnp.concatenate([residue, log_decay, short_weight.reshape(9, own)], 0)
    spread = jnp.broadcast_to(packed[None], (n_dev, rows, own))
    gathered = lax.all_to_all(spread, devices, 0, 0, tiled=True)
    par = gathered.transpose(1, 0, 2).reshape(rows, channels)

    signal = proj[0].transpose(1, 0, 2)
    upstream = cotangent[0]
    right = lambda k: [(i, i + k) for i in range(n_ctx - k)]
    left = lambda k: [(i + k, i) for i in range(n_ctx - k)]
    above = lax.ppermute(signal[:, chunk - 8 :], ctx, right(1))
    below = lax.ppermute(signal[:, :8], ctx, left(1))
    cot_below = lax.ppermute(upstream[:8], ctx, left(1))

    def spec(*shape):
        lead = len(shape) - 1
        return pl.BlockSpec(shape[:-1] + (block,), lambda i, lead=lead: (0,) * lead + (i,))

    def fixed(array):
        return pl.BlockSpec(array.shape, lambda i: (0, 0))

    def shape(dims, kind):
        return jax.ShapeDtypeStruct(dims, kind)

    wide = lambda n=chunk: pltpu.VMEM((n, block), F32)
    params = pltpu.CompilerParams(vmem_limit_bytes=48 * 1024 * 1024)
    gated, gate_grad, state, sent = pl.pallas_call(
        state_kernel,
        grid=grid,
        in_specs=[spec(3, chunk, 0), spec(3, 8, 0), spec(chunk, 0), spec(rows, 0)]
        + [fixed(rev2), fixed(sums), fixed(ramp)],
        out_specs=[spec(chunk, 0), spec(chunk, 0), spec(4 * ORDER, 0), spec(2, ORDER, 0)],
        out_shape=[
            shape((chunk, channels), BF),
            shape((chunk, channels), BF),
            shape((4 * ORDER, channels), F32),
            shape((2, ORDER, channels), BF),
        ],
        scratch_shapes=[wide(), wide()] + [wide(8 * ORDER)] * 4,
        compiler_params=params,
        name="states",
    )(signal, above, upstream, par, rev2, sums, ramp)

    before = jnp.stack([lax.ppermute(sent[0], ctx, right(k)) for k in range(1, n_ctx)])
    after = jnp.stack([lax.ppermute(sent[1], ctx, left(k)) for k in range(1, n_ctx)])

    conv, back, modal = pl.pallas_call(
        local_kernel,
        grid=grid,
        in_specs=[spec(chunk, 0), spec(chunk, 0), spec(rows, 0)]
        + [fixed(t) for t in (fwd2, inv_hi, inv_lo, sums, ramp)],
        out_specs=[spec(chunk, 0), spec(chunk, 0), spec(2 * ORDER, 0)],
        out_shape=[
            shape((chunk, channels), F32),
            shape((chunk, channels), F32),
            shape((2 * ORDER, channels), F32),
        ],
        scratch_shapes=[wide(), wide()] + [wide(8 * ORDER)] * 2,
        compiler_params=params,
        name="local",
    )(gated, gate_grad, par, fwd2, inv_hi, inv_lo, sums, ramp)

    out, proj_grad, grads = pl.pallas_call(
        final_kernel,
        grid=grid,
        in_specs=[
            spec(3, chunk, 0), spec(3, 8, 0), spec(3, 8, 0), spec(chunk, 0), spec(8, 0), spec(rows, 0),
            spec(4 * ORDER, 0), spec(n_ctx - 1, ORDER, 0), spec(n_ctx - 1, ORDER, 0),
            spec(2 * ORDER, 0), spec(chunk, 0), spec(chunk, 0), fixed(rev2),
        ],
        out_specs=[spec(chunk, 0), spec(3, chunk, 0), spec(rows, 0)],
        out_shape=[
            shape((chunk, channels), BF),
            shape((3, chunk, channels), BF),
            shape((rows, channels), F32),
        ],
        scratch_shapes=[wide(), wide()],
        compiler_params=params,
        name="final",
    )(signal, above, below, upstream, cot_below, par, state, before, after, modal, conv, back, rev2)

    parts = grads.reshape(rows, n_dev, own).transpose(1, 0, 2)
    arrived = lax.all_to_all(parts, devices, 0, 0, tiled=True)
    total = jnp.sum(arrived, axis=0) * (1.0 / seq)
    residue_grad = total[:ORDER]
    decay_grad = -residue * jnp.exp(log_decay) * total[ORDER : 2 * ORDER]
    tap_grad = total[2 * ORDER :].reshape(3, SHORT, own)
    return (
        out[None],
        proj_grad.transpose(1, 0, 2)[None],
        tap_grad,
        residue_grad,
        decay_grad,
    )


def solution(mesh):
    both = ("ctx", "zero")
    specs = (
        P("zero", "ctx", None, None),
        P(None, None, both),
        P(None, both),
        P(None, both),
        P("zero", "ctx", None),
    )
    out_specs = (specs[4], specs[0], specs[1], specs[2], specs[2])
    names = ("ctx", both, mesh.shape["ctx"])
    return jax.shard_map(
        functools.partial(body, names), mesh=mesh, in_specs=specs, out_specs=out_specs, check_vma=False
    )
```

```python
import functools

import jax
import jax.numpy as jnp
import ml_dtypes
import numpy as np
from jax import lax
from jax.experimental import pallas as pl
from jax.experimental.pallas import tpu as pltpu
from jax.sharding import PartitionSpec as P

SHORT = 3
ORDER = 16
WIRE = 16
WIRE_ROWS = 72
LANES = 128
BF = jnp.bfloat16
F32 = jnp.float32


def split_table(table):
    high = table.astype(ml_dtypes.bfloat16)
    low = (table - high.astype(np.float64)).astype(ml_dtypes.bfloat16)
    return high, low


def tables(chunk):
    padded = 2 * chunk
    index = np.arange(chunk)
    angle = 2.0 * np.pi / padded * (np.outer(index, index) % padded)
    parity = np.where(index % 2 == 0, 1.0, -1.0)
    cosine, sine = np.cos(angle), np.sin(angle)
    sine[0] = parity
    forward = np.concatenate([cosine, sine], 0)
    weight = np.where(index == 0, 1.0, 2.0) / padded
    backward = np.concatenate([cosine * weight[:, None], sine * weight[:, None]], 0).T
    fwd_hi, fwd_lo = split_table(forward)
    inv_hi, inv_lo = split_table(backward)
    fwd2 = np.concatenate([fwd_hi, fwd_lo], 1)
    reverse = np.eye(chunk)[::-1].astype(ml_dtypes.bfloat16)
    rev2 = np.concatenate([reverse, reverse], 1)
    inv2 = np.concatenate([inv_hi, inv_lo], 0)
    return fwd2, inv2, rev2


def mxu(left, right):
    return jnp.dot(left, right, preferred_element_type=F32)


def tree(parts):
    parts = list(parts)
    while len(parts) > 1:
        parts = [a + b for a, b in zip(parts[::2], parts[1::2])]
    return parts[0]


def halves(values):
    high = values.astype(BF)
    return high, (values - high.astype(F32)).astype(BF)


def down(values, above, offset):
    if offset == 0:
        return values
    rows = values.shape[0]
    return jnp.concatenate([above, values], 0)[8 - offset : 8 - offset + rows]


def up(values, below, offset):
    if offset == 0:
        return values
    rows = values.shape[0]
    return jnp.concatenate([values, below], 0)[offset : offset + rows]


def taps(values, above, weights, which):
    total = weights[3 * which][None] * values
    for offset in range(1, SHORT):
        total = total + weights[3 * which + offset][None] * down(values, above, offset)
    return total


def first_powers(rate):
    steps = lax.broadcasted_iota(jnp.int32, (8, LANES), 0).astype(F32)
    rates = jnp.broadcast_to(rate, (8, LANES))
    return jnp.exp(-rates * steps), jnp.exp(-8.0 * rates)


def fold(values):
    row = lax.broadcasted_iota(jnp.int32, (8, LANES), 0)
    for bit in (4, 2, 1):
        low = (row & bit) == 0
        made = []
        for one, two in zip(values[:bit], values[bit:]):
            kept = jnp.where(low, one, two)
            other = jnp.where(low, two, one)
            if bit == 4:
                moved = pltpu.roll(other, 4, 0)
            else:
                moved = jnp.where(low, pltpu.roll(other, 8 - bit, 0), pltpu.roll(other, bit, 0))
            made.append(kept + moved)
        values = made
    return values[0]


def swap_blocks(tile):
    row = lax.broadcasted_iota(jnp.int32, (8, LANES), 0)
    column = lax.broadcasted_iota(jnp.int32, (8, LANES), 1) // WIRE
    for bit in (1, 2, 4):
        row_bit, column_bit = row & bit, column & bit
        ahead = pltpu.roll(pltpu.roll(tile, 8 - bit, 0), WIRE * bit, 1)
        back = pltpu.roll(pltpu.roll(tile, bit, 0), LANES - WIRE * bit, 1)
        tile = jnp.where(row_bit == column_bit, tile, jnp.where(row_bit < column_bit, ahead, back))
    return tile


def moments(par_ref, sources, outs, lanes, tiles):
    place = lax.broadcasted_iota(jnp.int32, (8, LANES), 0).astype(F32) + 8.0 * (tiles - 1)
    for group in range(0, ORDER, 8):
        rates = [jnp.exp(par_ref[ORDER + m : ORDER + m + 1, lanes]) for m in range(group, group + 8)]
        powers, steps = map(list, zip(*[first_powers(r) for r in rates]))
        plain = [[None] * 8 for _ in sources]
        summed = [[None] * 8 for _ in sources]
        for tile in range(tiles):
            rows = slice(8 * tile, 8 * tile + 8)
            values = [s[rows, lanes] for s in sources]
            for g in range(8):
                for s, value in enumerate(values):
                    term = powers[g] * value
                    if tile == 0:
                        plain[s][g] = term
                        summed[s][g] = term
                    else:
                        plain[s][g] = plain[s][g] + term
                        if tile < tiles - 1:
                            summed[s][g] = summed[s][g] + plain[s][g]
                if tile < tiles - 1:
                    powers[g] = powers[g] * steps[g]
        for s, (ref, first_row) in enumerate(outs):
            ref[first_row + group : first_row + group + 8, lanes] = fold(plain[s])
            weighted = [place * p - 8.0 * q for p, q in zip(plain[s], summed[s])]
            ref[first_row + ORDER + group : first_row + ORDER + group + 8, lanes] = fold(weighted)


def state_kernel(
    where, proj, above, cot, wire, rev2, gated_out, grad_out, par, state_out, send1, send2, send3, xrev, grads
):
    chunk, block = cot.shape
    tiles = chunk // 8
    arrived = wire[...].astype(F32)
    for group in range(block // LANES):
        lanes = slice(group * LANES, group * LANES + LANES)
        parts = [
            swap_blocks(arrived[8 * group : 8 * group + 8, q * LANES : q * LANES + LANES])
            for q in range(WIRE_ROWS // 8)
        ]
        par[0:8, lanes] = parts[4]
        par[8:16, lanes] = parts[5]
        par[16:24, lanes] = parts[0] + parts[2]
        par[24:32, lanes] = parts[1] + parts[3]
        par[32:40, lanes] = parts[6] + parts[8]
        par[40:48, lanes] = jnp.broadcast_to(parts[7][0:1] + parts[7][1:2], (8, LANES))
    weights = [par[2 * ORDER + i] for i in range(9)]
    filtered = [
        taps(proj[i].astype(F32), above[i].astype(F32), weights, i) for i in range(3)
    ]
    gated = (filtered[1] * filtered[2]).astype(BF)
    gate_grad = (cot[...].astype(F32) * filtered[0]).astype(BF)
    gated_out[...] = gated
    grad_out[...] = gate_grad
    grads[...] = gate_grad.astype(F32)
    xrev[...] = mxu(rev2[:, :chunk], gated)

    @pl.loop(0, block // LANES)
    def _(step):
        lanes = pl.ds(pl.multiple_of(step * LANES, LANES), LANES)
        moments(par, [xrev, grads], [(state_out, 0), (state_out, 32)], lanes, tiles)

    forward, backward = state_out[0:16], state_out[32:48]
    for away, send in zip((1, 2, 3), (send1, send2, send3)):
        send[...] = jnp.where(where[0] + away < 4, forward, backward).astype(BF)


def local_kernel(
    gated, grad, par, fwd2, inv2, conv_out, back_out, modal_out, kern, corr
):
    chunk, block = gated.shape
    tiles = chunk // 8

    @pl.loop(0, block // LANES)
    def _(step):
        lanes = pl.ds(pl.multiple_of(step * LANES, LANES), LANES)
        half = ORDER // 2
        for group in (0, half):
            modes = range(group, group + half)
            rates = [jnp.exp(par[ORDER + m : ORDER + m + 1, lanes]) for m in modes]
            powers, steps = map(list, zip(*[first_powers(r) for r in rates]))
            gains = [jnp.broadcast_to(par[m : m + 1, lanes], (8, LANES)) for m in modes]
            powers = [p * g for p, g in zip(powers, gains)]
            for tile in range(tiles):
                rows = slice(8 * tile, 8 * tile + 8)
                total = tree(powers)
                if group:
                    total = total + kern[rows, lanes]
                kern[rows, lanes] = total
                powers = [p * s for p, s in zip(powers, steps)]

    def transform(values):
        return mxu(fwd2[...], jnp.concatenate([values, values], 0))

    def inverse(values):
        high, low = halves(values)
        both = mxu(inv2[...], high)
        return both[:chunk] + both[chunk:] + mxu(inv2[:chunk], low)

    x, g = transform(gated[...]), transform(grad[...])
    k_hi, k_lo = halves(kern[...])
    k = transform(k_hi) + mxu(fwd2[:, :chunk], k_lo)
    first = lax.broadcasted_iota(jnp.int32, (chunk, block), 0) == 0

    def product(a, b, sign):
        a_re, a_im, b_re, b_im = a[:chunk], a[chunk:], b[:chunk], b[chunk:]
        both = a_im * b_im
        real = a_re * b_re + jnp.where(first, 0.0, -sign * both)
        imag = jnp.where(first, both, a_re * b_im + sign * (a_im * b_re))
        return jnp.concatenate([real, imag], 0)

    conv_out[...] = inverse(product(k, x, 1.0))
    back_out[...] = inverse(product(k, g, -1.0))
    corr[...] = inverse(product(x, g, -1.0))

    @pl.loop(0, block // LANES)
    def _(step):
        lanes = pl.ds(pl.multiple_of(step * LANES, LANES), LANES)
        moments(par, [corr], [(modal_out, 0)], lanes, tiles)


def final_kernel(
    where, proj, above, below, cot, par, state, got1, got2, got3, modal, conv, back, rev2,
    out, proj_grad, sums_out, conv_x, back_x, grads,
):
    chunk, block = cot.shape
    tiles = chunk // 8
    residue = par[0:ORDER]
    rate = jnp.exp(par[ORDER : 2 * ORDER])
    one = jnp.exp(-rate)
    whole = jnp.exp(-float(chunk) * rate)
    entering = jnp.zeros_like(rate)
    leaving = jnp.zeros_like(rate)
    scales = [jnp.ones_like(rate), whole, whole * whole]
    for away, got in zip((1, 2, 3), (got1, got2, got3)):
        state_got = got[...].astype(F32)
        entering = entering + jnp.where(where[0] >= away, scales[away - 1] * state_got, 0.0)
        leaving = leaving + jnp.where(where[0] < away, scales[3 - away] * state_got, 0.0)
    s0, s1, p0, p1 = (state[16 * i : 16 * i + 16] for i in range(4))
    grads[0:16] = modal[0:16] + one * p0 * entering
    grads[16:32] = modal[16:32] + one * (
        p1 * entering + s1 * leaving + p0 * entering + chunk * whole * entering * leaving
    )
    in_gain = one * residue * entering
    out_gain = one * residue * leaving
    half = ORDER // 2
    for step in range(block // LANES):
        lanes = slice(step * LANES, step * LANES + LANES)
        for group in (0, half):
            modes = range(group, group + half)
            made = [first_powers(rate[m : m + 1, lanes]) for m in modes]
            powers, steps = map(list, zip(*made))
            gain_x = [jnp.broadcast_to(in_gain[m : m + 1, lanes], (8, LANES)) for m in modes]
            gain_g = [jnp.broadcast_to(out_gain[m : m + 1, lanes], (8, LANES)) for m in modes]
            for tile in range(tiles):
                rows = slice(8 * tile, 8 * tile + 8)
                sum_x = conv[rows, lanes] if group == 0 else conv_x[rows, lanes]
                sum_g = None if group == 0 else back_x[rows, lanes]
                new_x = tree([gx * p for p, gx in zip(powers, gain_x)])
                new_g = tree([gg * p for p, gg in zip(powers, gain_g)])
                conv_x[rows, lanes] = sum_x + new_x
                back_x[rows, lanes] = new_g if sum_g is None else sum_g + new_g
                if tile < tiles - 1:
                    powers = [p * s for p, s in zip(powers, steps)]

    weights = [par[2 * ORDER + i] for i in range(9)]
    signal = [proj[i].astype(F32) for i in range(3)]
    halo = [above[i].astype(F32) for i in range(3)]
    upstream = cot[...].astype(F32)
    queries, keys, values = (taps(signal[i], halo[i], weights, i) for i in range(3))
    convolved = conv_x[...].astype(BF).astype(F32)
    b_hi, b_lo = halves(back_x[...])
    crossed = mxu(rev2[...], jnp.concatenate([b_hi, b_lo], 0))
    gated_grad = (back[...] + crossed).astype(BF).astype(F32)
    out[...] = (queries * convolved).astype(BF)
    fgrad = [upstream * convolved, gated_grad * values, gated_grad * keys]

    tails = [below[i].astype(F32) for i in range(3)]
    q_r, k_r, v_r = (taps(tails[i], signal[i][chunk - 8 :], weights, i) for i in range(3))
    cot_r = below[3].astype(F32)
    x_r = (k_r * v_r).astype(BF).astype(F32)
    g_r = (cot_r * q_r).astype(BF).astype(F32)
    h0 = one * (whole * entering + s0) + x_r[0:1]
    h1 = one * h0 + x_r[1:2]
    e1 = (leaving - g_r[0:1]) / one
    rows8 = lax.broadcasted_iota(jnp.int32, (8, block), 0)

    def two_rows(a, b):
        a = jnp.sum(residue * a, axis=0, keepdims=True)
        b = jnp.sum(residue * b, axis=0, keepdims=True)
        both = jnp.where(rows8 == 0, a, jnp.where(rows8 == 1, b, 0.0))
        return both.astype(BF).astype(F32)

    conv_r, back_r = two_rows(h0, h1), two_rows(leaving, e1)
    fgrad_r = [cot_r * conv_r, back_r * v_r, back_r * k_r]

    lines = []
    for i in range(3):
        total = weights[3 * i][None] * fgrad[i]
        for offset in range(1, SHORT):
            total = total + weights[3 * i + offset][None] * up(fgrad[i], fgrad_r[i], offset)
        proj_grad[i] = total.astype(BF)
        for offset in range(SHORT):
            moved = down(signal[i], halo[i], offset)
            lines.append(jnp.sum(fgrad[i] * moved, axis=0, keepdims=True))
    for i in range(9):
        grads[2 * ORDER + i : 2 * ORDER + i + 1] = lines[i]
    grads[2 * ORDER + 9 :] = jnp.zeros((7, block), F32)
    rows_out = []
    for group in range(block // LANES):
        lanes = slice(group * LANES, group * LANES + LANES)
        rows_out.append(
            jnp.concatenate([swap_blocks(grads[8 * q : 8 * q + 8, lanes]) for q in range(6)], 1)
        )
    sums_out[...] = jnp.concatenate(rows_out, 0).astype(BF)


def body(names, proj, short_weight, residue, log_decay, cotangent):
    ctx, devices, n_ctx = names
    chunk, channels = cotangent.shape[1:]
    own = residue.shape[1]
    seq = chunk * n_ctx
    n_dev = channels // own
    block = 512 if channels % 512 == 0 else channels
    grid = (channels // block,)
    fwd2, inv2, rev2 = (jnp.asarray(t) for t in tables(chunk))
    where = lax.axis_index(ctx).astype(jnp.int32).reshape(1)

    weights = short_weight.reshape(9, own)
    exact = jnp.concatenate([log_decay, weights], 0)
    high = lax.optimization_barrier(exact.astype(BF))
    low = (exact - high.astype(F32)).astype(BF)
    packed = jnp.concatenate(
        [
            high[:16], low[:16], residue.astype(BF), high[16:24],
            high[24:], low[24:], jnp.zeros((6, own), BF), low[16:24],
        ],
        0,
    ).reshape(1, WIRE_ROWS * own)
    spread = jnp.broadcast_to(packed, (n_dev, WIRE_ROWS * own))
    wire = lax.all_to_all(spread, devices, 0, 0, tiled=True)

    signal = proj[0].transpose(1, 0, 2)
    upstream = cotangent[0]
    right = [(i, i + 1) for i in range(n_ctx - 1)]
    left = [(i + 1, i) for i in range(n_ctx - 1)]
    above = lax.ppermute(signal[:, chunk - 8 :], ctx, right)
    below = lax.ppermute(jnp.concatenate([signal[:, :8], upstream[None, :8]], 0), ctx, left)

    def spec(*shape):
        lead = len(shape) - 1
        return pl.BlockSpec(shape[:-1] + (block,), lambda i, lead=lead: (0,) * lead + (i,))

    def rows(count):
        return pl.BlockSpec((block // own, count), lambda i: (i, 0))

    def fixed(array):
        return pl.BlockSpec(array.shape, lambda i: (0, 0))

    def shape(dims, kind):
        return jax.ShapeDtypeStruct(dims, kind)

    scalar = pl.BlockSpec(memory_space=pltpu.SMEM)
    wide = lambda n=chunk: pltpu.VMEM((n, block), F32)
    params = pltpu.CompilerParams(vmem_limit_bytes=48 * 1024 * 1024)
    sent = [shape((ORDER, channels), BF)] * 3
    gated, gate_grad, par, state, *sent = pl.pallas_call(
        state_kernel,
        grid=grid,
        in_specs=[scalar, spec(3, chunk, 0), spec(3, 8, 0), spec(chunk, 0), rows(WIRE_ROWS * own), fixed(rev2)],
        out_specs=[spec(chunk, 0), spec(chunk, 0), spec(48, 0), spec(4 * ORDER, 0)] + [spec(ORDER, 0)] * 3,
        out_shape=[
            shape((chunk, channels), BF),
            shape((chunk, channels), BF),
            shape((48, channels), F32),
            shape((4 * ORDER, channels), F32),
        ]
        + sent,
        scratch_shapes=[wide(), wide()],
        compiler_params=params,
        name="states",
    )(where, signal, above, upstream, wire, rev2)

    got = [
        lax.ppermute(values, ctx, [(i, (i + k) % n_ctx) for i in range(n_ctx)])
        for k, values in zip((1, 2, 3), sent)
    ]

    conv, back, modal = pl.pallas_call(
        local_kernel,
        grid=grid,
        in_specs=[spec(chunk, 0), spec(chunk, 0), spec(48, 0), fixed(fwd2), fixed(inv2)],
        out_specs=[spec(chunk, 0), spec(chunk, 0), spec(2 * ORDER, 0)],
        out_shape=[
            shape((chunk, channels), F32),
            shape((chunk, channels), F32),
            shape((2 * ORDER, channels), F32),
        ],
        scratch_shapes=[wide(), wide()],
        compiler_params=params,
        cost_estimate=pl.CostEstimate(flops=8 * 10**9, bytes_accessed=10**7, transcendentals=0),
        name="local",
    )(gated, gate_grad, par, fwd2, inv2)

    out, proj_grad, parts = pl.pallas_call(
        final_kernel,
        grid=grid,
        in_specs=[
            scalar, spec(3, chunk, 0), spec(3, 8, 0), spec(4, 8, 0), spec(chunk, 0), spec(48, 0),
            spec(4 * ORDER, 0), spec(ORDER, 0), spec(ORDER, 0), spec(ORDER, 0),
            spec(2 * ORDER, 0), spec(chunk, 0), spec(chunk, 0), fixed(rev2),
        ],
        out_specs=[spec(chunk, 0), spec(3, chunk, 0), rows(48 * own)],
        out_shape=[
            shape((chunk, channels), BF),
            shape((3, chunk, channels), BF),
            shape((n_dev, 48 * own), BF),
        ],
        scratch_shapes=[wide(), wide(), wide(48)],
        compiler_params=params,
        name="final",
    )(where, signal, above, below, upstream, par, state, *got, modal, conv, back, rev2)

    arrived = lax.all_to_all(parts, devices, 0, 0, tiled=True)
    total = jnp.sum(arrived.astype(F32), axis=0) * (1.0 / seq)
    total = total.reshape(48, own)
    residue_grad = total[:ORDER]
    decay_grad = -residue * jnp.exp(log_decay) * total[ORDER : 2 * ORDER]
    tap_grad = total[2 * ORDER : 2 * ORDER + 9].reshape(3, SHORT, own)
    return (
        out[None],
        proj_grad.transpose(1, 0, 2)[None],
        tap_grad,
        residue_grad,
        decay_grad,
    )


def solution(mesh):
    both = ("ctx", "zero")
    specs = (
        P("zero", "ctx", None, None),
        P(None, None, both),
        P(None, both),
        P(None, both),
        P("zero", "ctx", None),
    )
    out_specs = (specs[4], specs[0], specs[1], specs[2], specs[2])
    names = ("ctx", both, mesh.shape["ctx"])
    return jax.shard_map(
        functools.partial(body, names), mesh=mesh, in_specs=specs, out_specs=out_specs, check_vma=False
    )
```

```python
import functools

import jax
import jax.numpy as jnp
from jax import lax
from jax.experimental import pallas as pl
from jax.experimental.pallas import tpu as pltpu
from jax.sharding import PartitionSpec as P

SHORT = 3
ORDER = 16
LANES = 128
WIDE = 8 * LANES
WIRE = 16
WIRE_ROWS = 72
SUM_ROWS = 48
HALF = ORDER // 2
BF = jnp.bfloat16
F32 = jnp.float32


def tree(parts):
    parts = list(parts)
    while len(parts) > 1:
        parts = [a + b for a, b in zip(parts[::2], parts[1::2])]
    return parts[0]


def rounded(values):
    return values.astype(BF).astype(F32)


def swap_blocks(tile):
    row = lax.broadcasted_iota(jnp.int32, (8, LANES), 0)
    column = lax.broadcasted_iota(jnp.int32, (8, LANES), 1) // WIRE
    for bit in (1, 2, 4):
        row_bit, column_bit = row & bit, column & bit
        ahead = pltpu.roll(pltpu.roll(tile, 8 - bit, 0), WIRE * bit, 1)
        back = pltpu.roll(pltpu.roll(tile, bit, 0), LANES - WIRE * bit, 1)
        tile = jnp.where(row_bit == column_bit, tile, jnp.where(row_bit < column_bit, ahead, back))
    return tile


def tile_rows(tile, lane):
    start = (tile * 8 + lane) * 8
    return pl.ds(start if isinstance(start, int) else pl.multiple_of(start, 8), 8)


def line_rows(row):
    return pl.ds((row // 8) * 64 + row % 8, 8, stride=8)


def tap_weights(par, lane):
    first = par[tile_rows(4, lane), :]
    last = par[tile_rows(5, lane), :]
    return [first[i : i + 1] for i in range(8)] + [last[0:1]]


def column(lane):
    return pl.ds(pl.multiple_of(lane * LANES, LANES), LANES)


def load_signal(which, proj, above, signal, lane):
    rows = proj.shape[1]
    signal[which, 0:8] = above[which, :, column(lane)].astype(F32)
    signal[which, 8 : 8 + rows] = proj[which, :, column(lane)].astype(F32)


def taps(which, signal, weights, start, rows):
    return tree(
        [weights[3 * which + j] * signal[which, 8 + start - j : 8 + start - j + rows] for j in range(2)]
    ) + weights[3 * which + 2] * signal[which, 6 + start : 6 + start + rows]


def decay_of(par):
    return [jnp.exp(-jnp.exp(par[line_rows(ORDER + m), :])) for m in range(ORDER)]


def flat_row(rows):
    padded = jnp.concatenate([rows, jnp.zeros((8, LANES - WIRE), F32)], 1)
    return swap_blocks(padded)[0:1]


def spread_kernel(short_weight, residue, log_decay, out):
    weights = jnp.concatenate([short_weight[i] for i in range(3)], 0)
    rates = log_decay[...]
    rates_high, weights_high = rounded(rates), rounded(weights)
    rates_low, weights_low = rates - rates_high, weights - weights_high
    last = jnp.concatenate([weights_high[8:], weights_low[8:], jnp.zeros((6, WIRE), F32)], 0)
    tiles = [
        rates_high[:8], rates_high[8:], rates_low[:8], rates_low[8:], residue[:8], residue[8:],
        weights_high[:8], last, weights_low[:8],
    ]
    for q, tile in enumerate(tiles):
        row = jnp.broadcast_to(flat_row(tile), (out.shape[0], LANES))
        out[:, q * LANES : q * LANES + LANES] = row.astype(BF)


def collect_kernel(scale, arrived, residue, log_decay, tap_grad, residue_grad, decay_grad):
    total = jnp.sum(arrived[...].astype(F32), axis=0, keepdims=True) * scale
    first = lax.broadcasted_iota(jnp.int32, (8, LANES), 0) == 0
    tiles = [
        swap_blocks(jnp.where(first, total[:, q * LANES : q * LANES + LANES], 0.0))[:, :WIRE]
        for q in range(SUM_ROWS // 8)
    ]
    residue_grad[...] = jnp.concatenate(tiles[0:2], 0)
    decay_grad[...] = -residue[...] * jnp.exp(log_decay[...]) * jnp.concatenate(tiles[2:4], 0)
    lines = jnp.concatenate(tiles[4:6], 0)
    for i in range(3):
        tap_grad[i] = lines[3 * i : 3 * i + 3]


def state_kernel(where, proj, above, cot, wire, par, send1, send2, send3, signal, xs, gs):
    chunk = cot.shape[0]
    arrived = wire[...].astype(F32)
    for lane in range(8):
        parts = [
            swap_blocks(arrived[8 * lane : 8 * lane + 8, q * LANES : q * LANES + LANES])
            for q in range(WIRE_ROWS // 8)
        ]
        par[tile_rows(0, lane), :] = parts[4]
        par[tile_rows(1, lane), :] = parts[5]
        par[tile_rows(2, lane), :] = parts[0] + parts[2]
        par[tile_rows(3, lane), :] = parts[1] + parts[3]
        par[tile_rows(4, lane), :] = parts[6] + parts[8]
        par[tile_rows(5, lane), :] = jnp.broadcast_to(parts[7][0:1] + parts[7][1:2], (8, LANES))

    @pl.loop(0, 8)
    def _(lane):
        weights = tap_weights(par, lane)
        for i in range(3):
            load_signal(i, proj, above, signal, lane)
        queries, keys, values = (taps(i, signal, weights, 0, chunk) for i in range(3))
        gated = rounded(keys * values)
        gate_grad = rounded(cot[:, column(lane)].astype(F32) * queries)
        for tile in range(chunk // 8):
            xs[tile_rows(tile, lane), :] = gated[8 * tile : 8 * tile + 8]
            gs[tile_rows(tile, lane), :] = gate_grad[8 * tile : 8 * tile + 8]

    decay = decay_of(par)

    def step(tile, carry):
        forward, backward = map(list, carry)
        for i in range(8):
            x = xs[pl.ds(tile * 64 + i, 8, stride=8), :]
            g = gs[pl.ds((chunk // 8 - 1 - tile) * 64 + 7 - i, 8, stride=8), :]
            forward = [a * h + x for a, h in zip(decay, forward)]
            backward = [a * p + g for a, p in zip(decay, backward)]
        return tuple(forward), tuple(backward)

    zero = tuple(jnp.zeros((8, LANES), F32) for _ in range(ORDER))
    forward, backward = lax.fori_loop(0, chunk // 8, step, (zero, zero))
    for away, send in zip((1, 2, 3), (send1, send2, send3)):
        ahead = where[0] + away < 4
        for m in range(0, ORDER, 2):
            pair = [jnp.where(ahead, forward[n], backward[n]) for n in (m, m + 1)]
            send[8 * m : 8 * m + 16, :] = jnp.concatenate(pair, 0).astype(BF)


def final_kernel(*refs):
    (where, proj, above, below, cot, par, got1, got2, got3, *rest) = refs
    (out, proj_grad, sums_out, signal, tails, fgrads, xs, gs, ys, bs, queries_s, keys_s, values_s, held, sums) = rest[-15:]
    chunk = cot.shape[0]
    tiles = chunk // 8

    @pl.loop(0, 8)
    def _(lane):
        weights = tap_weights(par, lane)
        for i in range(3):
            load_signal(i, proj, above, signal.at[lane], lane)
            signal[lane, i, 8 + chunk :] = below[i, :, column(lane)].astype(F32)
        here = signal.at[lane]
        queries, keys, values = (taps(i, here, weights, 0, chunk + 8) for i in range(3))
        gated = rounded(keys * values)
        queries_s[lane] = queries
        keys_s[lane] = keys
        values_s[lane] = values
        for tile in range(tiles + 1):
            rows = slice(8 * tile, 8 * tile + 8)
            if tile < tiles:
                upstream = cot[rows, column(lane)].astype(F32)
            else:
                upstream = below[3, :, column(lane)].astype(F32)
            xs[tile_rows(tile, lane), :] = gated[rows]
            gs[tile_rows(tile, lane), :] = rounded(upstream * queries[rows])

    for group in range(0, ORDER, HALF):
        modes = range(group, group + HALF)
        rates = [jnp.exp(par[line_rows(ORDER + m), :]) for m in modes]
        decay = [jnp.exp(-r) for r in rates]
        gain = [par[line_rows(m), :] for m in modes]
        entering, leaving = [], []
        for n, m in enumerate(modes):
            whole = jnp.exp(-float(chunk) * rates[n])
            scales = [None, whole, whole * whole]
            enter, leave = jnp.zeros((8, LANES), F32), jnp.zeros((8, LANES), F32)
            for away, got in zip((1, 2, 3), (got1, got2, got3)):
                pair = got[16 * (m // 2) : 16 * (m // 2) + 16, :].astype(F32)
                state = pair[8 * (m % 2) : 8 * (m % 2) + 8]
                near = state if away == 1 else scales[away - 1] * state
                far = state if away == 3 else scales[3 - away] * state
                enter = enter + jnp.where(where[0] >= away, near, 0.0)
                leave = leave + jnp.where(where[0] < away, far, 0.0)
            entering.append(enter)
            leaving.append(leave)

        def store(ref, rows, value, group=group):
            if group:
                value = value + ref[rows, :]
            ref[rows, :] = value

        def forward(tile, carry):
            states, totals = map(list, carry)
            for i in range(8):
                rows = pl.ds(tile * 64 + i, 8, stride=8)
                x, g = xs[rows, :], gs[rows, :]
                for n in range(HALF):
                    held[tile * 8 + i, n] = states[n]
                states = [a * h + x for a, h in zip(decay, states)]
                totals = [t + g * h for t, h in zip(totals, states)]
                store(ys, rows, tree([r * h for r, h in zip(gain, states)]))
            return tuple(states), tuple(totals)

        zero = tuple(jnp.zeros((8, LANES), F32) for _ in modes)
        states, totals = lax.fori_loop(0, tiles, forward, (tuple(entering), zero))
        for i in range(2):
            rows = line_rows(chunk + i)
            states = [a * h + xs[rows, :] for a, h in zip(decay, states)]
            store(ys, rows, tree([r * h for r, h in zip(gain, states)]))

        def backward(step, carry):
            states, counts = map(list, carry)
            tile = tiles - 1 - step
            for i in range(7, -1, -1):
                rows = pl.ds(tile * 64 + i, 8, stride=8)
                g = gs[rows, :]
                states = [a * p + g for a, p in zip(decay, states)]
                counts = [c + p * held[tile * 8 + i, n] for n, (c, p) in enumerate(zip(counts, states))]
                store(bs, rows, tree([r * p for r, p in zip(gain, states)]))
            return tuple(states), tuple(counts)

        _, counts = lax.fori_loop(0, tiles, backward, (tuple(leaving), zero))
        store(bs, line_rows(chunk), tree([r * p for r, p in zip(gain, leaving)]))
        after = [(p - gs[line_rows(chunk), :]) / a for a, p in zip(decay, leaving)]
        store(bs, line_rows(chunk + 1), tree([r * p for r, p in zip(gain, after)]))
        for n, m in enumerate(modes):
            sums[line_rows(m), :] = totals[n]
            sums[line_rows(ORDER + m), :] = decay[n] * counts[n]

    two = lax.broadcasted_iota(jnp.int32, (8, LANES), 0) < 2

    @pl.loop(0, 8)
    def _(lane):
        weights = tap_weights(par, lane)
        upstream = cot[:, column(lane)].astype(F32)
        tail_up = below[3, :, column(lane)].astype(F32)
        convolved = rounded(jnp.concatenate([ys[tile_rows(t, lane), :] for t in range(tiles)], 0))
        gated_grad = rounded(jnp.concatenate([bs[tile_rows(t, lane), :] for t in range(tiles)], 0))
        tail_conv = rounded(jnp.where(two, ys[tile_rows(tiles, lane), :], 0.0))
        tail_back = rounded(jnp.where(two, bs[tile_rows(tiles, lane), :], 0.0))
        out[:, column(lane)] = (queries_s[lane, 0:chunk] * convolved).astype(BF)
        lines = []
        for i in range(3):
            if i == 0:
                grad, tail = upstream * convolved, tail_up * tail_conv
            else:
                other = values_s if i == 1 else keys_s
                grad = gated_grad * other[lane, 0:chunk]
                tail = tail_back * other[lane, chunk : chunk + 8]
            fgrads[i, 0:chunk] = grad
            fgrads[i, chunk:] = tail
            total = weights[3 * i] * grad
            for j in range(1, SHORT):
                total = total + weights[3 * i + j] * fgrads[i, j : j + chunk]
            proj_grad[i, :, column(lane)] = total.astype(BF)
            for j in range(SHORT):
                lines.append(jnp.sum(grad * signal[lane, i, 8 - j : 8 - j + chunk], axis=0, keepdims=True))
        sums[tile_rows(4, lane), :] = jnp.concatenate(lines[:8], 0)
        sums[tile_rows(5, lane), :] = jnp.concatenate([lines[8], jnp.zeros((7, LANES), F32)], 0)

    for lane in range(0, 8, 2):
        rows = [
            jnp.concatenate([swap_blocks(sums[tile_rows(q, k), :]) for q in range(SUM_ROWS // 8)], 1)
            for k in (lane, lane + 1)
        ]
        sums_out[8 * lane : 8 * lane + 16, :] = jnp.concatenate(rows, 0).astype(BF)


def body(names, proj, short_weight, residue, log_decay, cotangent):
    ctx, devices, n_ctx = names
    chunk, channels = cotangent.shape[1:]
    own = residue.shape[1]
    seq = chunk * n_ctx
    n_dev = channels // own
    blocks = channels // WIDE
    runs = 2 if blocks % 2 == 0 else 1
    steps = blocks // runs
    where = lax.axis_index(ctx).astype(jnp.int32).reshape(1)

    spread = pl.pallas_call(
        spread_kernel,
        out_shape=jax.ShapeDtypeStruct((n_dev, WIRE_ROWS * own), BF),
        name="spread",
    )(short_weight, residue, log_decay)
    wire = lax.all_to_all(spread, devices, 0, 0, tiled=True)

    signal = proj[0].transpose(1, 0, 2)
    upstream = cotangent[0]
    right = [(i, i + 1) for i in range(n_ctx - 1)]
    left = [(i + 1, i) for i in range(n_ctx - 1)]
    above = lax.ppermute(signal[:, chunk - 8 :], ctx, right)
    below = lax.ppermute(jnp.concatenate([signal[:, :8], upstream[None, :8]], 0), ctx, left)

    def shape(dims, kind):
        return jax.ShapeDtypeStruct(dims, kind)

    scalar = pl.BlockSpec(memory_space=pltpu.SMEM)
    anywhere = pl.BlockSpec(memory_space=pl.ANY)
    vmem = lambda *dims: pltpu.VMEM(dims, F32)
    params = pltpu.CompilerParams(vmem_limit_bytes=48 * 1024 * 1024)

    def specs(run):
        def wide(*dims):
            lead = len(dims)
            return pl.BlockSpec(dims + (WIDE,), lambda i: (0,) * lead + (i + run * steps,))

        def rows(count):
            return pl.BlockSpec((WIDE // own, count), lambda i: (i + run * steps, 0))

        def whole(count):
            return pl.BlockSpec((None, count, LANES), lambda i: (i, 0, 0))

        return wide, rows, whole

    pars, gots = [], []
    for run in range(runs):
        wide, rows, whole = specs(run)
        par, *sent = pl.pallas_call(
            state_kernel,
            grid=(steps,),
            in_specs=[scalar, wide(3, chunk), wide(3, 8), wide(chunk), rows(WIRE_ROWS * own)],
            out_specs=[whole(8 * SUM_ROWS)] + [whole(8 * ORDER)] * 3,
            out_shape=[shape((steps, 8 * SUM_ROWS, LANES), F32)]
            + [shape((steps, 8 * ORDER, LANES), BF)] * 3,
            scratch_shapes=[vmem(3, chunk + 8, LANES), vmem(chunk * 8, LANES), vmem(chunk * 8, LANES)],
            compiler_params=params,
            cost_estimate=pl.CostEstimate(flops=4 * 10**9, bytes_accessed=4 * 10**6, transcendentals=0),
            name="states",
        )(where, signal, above, upstream, wire)
        pars.append(par)
        gots.append(
            [
                lax.ppermute(values, ctx, [(i, (i + k) % n_ctx) for i in range(n_ctx)])
                for k, values in zip((1, 2, 3), sent)
            ]
        )

    results = [
        shape((chunk, channels), BF),
        shape((3, chunk, channels), BF),
        shape((n_dev, SUM_ROWS * own), BF),
    ]
    made = []
    longer = chunk + 8
    for run in range(runs):
        wide, rows, whole = specs(run)
        made = pl.pallas_call(
            final_kernel,
            grid=(steps,),
            in_specs=[scalar, wide(3, chunk), wide(3, 8), wide(4, 8), wide(chunk), whole(8 * SUM_ROWS)]
            + [whole(8 * ORDER)] * 3
            + [anywhere] * len(made),
            out_specs=[wide(chunk), wide(3, chunk), rows(SUM_ROWS * own)],
            out_shape=results,
            scratch_shapes=[
                vmem(8, 3, chunk + 16, LANES), vmem(8, LANES), vmem(3, longer, LANES),
                vmem(longer * 8, LANES), vmem(longer * 8, LANES),
                vmem(longer * 8, LANES), vmem(longer * 8, LANES),
                vmem(8, longer, LANES), vmem(8, longer, LANES), vmem(8, longer, LANES),
                vmem(chunk, HALF, 8, LANES), vmem(8 * SUM_ROWS, LANES),
            ],
            input_output_aliases={9 + i: i for i in range(len(made))},
            compiler_params=params,
            cost_estimate=pl.CostEstimate(flops=8 * 10**9, bytes_accessed=8 * 10**6, transcendentals=0),
            name="final",
        )(where, signal, above, below, upstream, pars[run], *gots[run], *made)
    out, proj_grad, parts = made

    arrived = lax.all_to_all(parts, devices, 0, 0, tiled=True)
    tap_grad, residue_grad, decay_grad = pl.pallas_call(
        functools.partial(collect_kernel, 1.0 / seq),
        out_shape=[shape((3, SHORT, own), F32), shape((ORDER, own), F32), shape((ORDER, own), F32)],
        name="collect",
    )(arrived, residue, log_decay)
    return (
        out[None],
        proj_grad.transpose(1, 0, 2)[None],
        tap_grad,
        residue_grad,
        decay_grad,
    )


def solution(mesh):
    both = ("ctx", "zero")
    specs = (
        P("zero", "ctx", None, None),
        P(None, None, both),
        P(None, both),
        P(None, both),
        P("zero", "ctx", None),
    )
    out_specs = (specs[4], specs[0], specs[1], specs[2], specs[2])
    names = ("ctx", both, mesh.shape["ctx"])
    return jax.shard_map(
        functools.partial(body, names), mesh=mesh, in_specs=specs, out_specs=out_specs, check_vma=False
    )
```

```python
import functools

import jax
import jax.numpy as jnp
from jax import lax
from jax.experimental import pallas as pl
from jax.experimental.pallas import tpu as pltpu
from jax.sharding import PartitionSpec as P

SHORT = 3
ORDER = 16
LANES = 128
WIDE = 8 * LANES
WIRE = 16
WIRE_ROWS = 64
SUM_ROWS = 48
PAR_ROWS = 48
RATE_CENTRE = -5.4
HALF = ORDER // 2
BF = jnp.bfloat16
F32 = jnp.float32


def tree(parts):
    parts = list(parts)
    while len(parts) > 1:
        parts = [a + b for a, b in zip(parts[::2], parts[1::2])]
    return parts[0]


def rounded(values):
    return values.astype(BF).astype(F32)


def turn_rows(tile, forward):
    if forward:
        return pltpu.roll(tile, 0, 1, stride=WIRE, stride_axis=0)
    row = lax.broadcasted_iota(jnp.int32, (8, LANES), 0)
    for bit in (1, 2, 4):
        tile = jnp.where((row & bit) != 0, pltpu.roll(tile, LANES - WIRE * bit, 1), tile)
    return tile


def turn_columns(tile, forward):
    column = lax.broadcasted_iota(jnp.int32, (8, LANES), 1) // WIRE
    for bit in (1, 2, 4):
        tile = jnp.where((column & bit) != 0, pltpu.roll(tile, bit if forward else 8 - bit, 0), tile)
    return tile


def rows_of_lines(tile):
    return turn_rows(turn_columns(turn_rows(tile, True), False), True)


def lines_of_rows(tile):
    return turn_rows(turn_columns(turn_rows(tile, False), True), False)


def wire_order(rows):
    return jnp.concatenate([rows[(8 - b) % 8 : (8 - b) % 8 + 1] for b in range(8)], 0)


def tile_rows(tile, lane):
    start = (tile * 8 + lane) * 8
    return pl.ds(start if isinstance(start, int) else pl.multiple_of(start, 8), 8)


def line_rows(row):
    return pl.ds((row // 8) * 64 + row % 8, 8, stride=8)


def tap_weights(par, lane):
    first = par[tile_rows(4, lane), :]
    last = par[tile_rows(5, lane), :]
    return [first[i : i + 1] for i in range(8)] + [last[0:1]]


def column(lane):
    return pl.ds(pl.multiple_of(lane * LANES, LANES), LANES)


def load_signal(which, proj, above, signal, lane):
    rows = proj.shape[1]
    signal[which, 0:8] = above[which, :, column(lane)].astype(F32)
    signal[which, 8 : 8 + rows] = proj[which, :, column(lane)].astype(F32)


def taps(which, signal, weights, start, rows):
    return tree(
        [weights[3 * which + j] * signal[which, 8 + start - j : 8 + start - j + rows] for j in range(2)]
    ) + weights[3 * which + 2] * signal[which, 6 + start : 6 + start + rows]


def decay_of(par):
    return [jnp.exp(-jnp.exp(par[line_rows(ORDER + m), :])) for m in range(ORDER)]


def flat_row(rows):
    padded = jnp.concatenate([wire_order(rows), jnp.zeros((8, LANES - WIRE), F32)], 1)
    return jnp.sum(turn_rows(padded, True), axis=0, keepdims=True)


def spread_kernel(short_weight, residue, log_decay, out):
    weights = jnp.concatenate([short_weight[i] for i in range(3)], 0)
    rates = log_decay[...] - RATE_CENTRE
    rates_high, weights_high = rounded(rates), rounded(weights)
    rates_low, weights_low = rates - rates_high, weights - weights_high
    tiles = [
        rates_high[:8], rates_high[8:], rates_low[:8],
        jnp.concatenate([rates_low[8:14], weights_high[8:], weights_low[8:]], 0),
        residue[:8], residue[8:], weights_high[:8], weights_low[:8],
    ]
    rows = jnp.concatenate([flat_row(tile) for tile in tiles], 0)
    out[...] = jnp.broadcast_to(rows[None], out.shape).astype(BF)


def collect_kernel(scale, arrived, residue, log_decay, tap_grad, residue_grad, decay_grad):
    total = jnp.sum(arrived[...].astype(F32), axis=0) * scale
    tiles = [
        wire_order(turn_rows(jnp.broadcast_to(total[q : q + 1], (8, LANES)), False)[:, :WIRE])
        for q in range(SUM_ROWS // 8)
    ]
    residue_grad[...] = jnp.concatenate(tiles[0:2], 0)
    decay_grad[...] = -residue[...] * jnp.exp(log_decay[...]) * jnp.concatenate(tiles[2:4], 0)
    lines = jnp.concatenate(tiles[4:6], 0)
    for i in range(3):
        tap_grad[i] = lines[3 * i : 3 * i + 3]


def state_kernel(where, proj, above, cot, wire, par, send1, send2, send3, signal, xs, gs, wires):
    chunk = cot.shape[0]
    wires[...] = wire[...].astype(F32).reshape(wires.shape)
    early = lax.broadcasted_iota(jnp.int32, (8, LANES), 0) < 6

    for lane in range(8):
        parts = [rows_of_lines(wires[pl.ds(lane * 64 + q, 8, stride=8), :]) for q in range(8)]
        par[tile_rows(0, lane), :] = parts[4]
        par[tile_rows(1, lane), :] = parts[5]
        par[tile_rows(2, lane), :] = parts[0] + parts[2] + RATE_CENTRE
        par[tile_rows(3, lane), :] = parts[1] + jnp.where(early, parts[3], 0.0) + RATE_CENTRE
        par[tile_rows(4, lane), :] = parts[6] + parts[7]
        par[tile_rows(5, lane), :] = jnp.broadcast_to(parts[3][6:7] + parts[3][7:8], (8, LANES))

    @pl.loop(0, 8)
    def _(lane):
        weights = tap_weights(par, lane)
        for i in range(3):
            load_signal(i, proj, above, signal, lane)
        queries, keys, values = (taps(i, signal, weights, 0, chunk) for i in range(3))
        gated = rounded(keys * values)
        gate_grad = rounded(cot[:, column(lane)].astype(F32) * queries)
        for tile in range(chunk // 8):
            xs[tile_rows(tile, lane), :] = gated[8 * tile : 8 * tile + 8]
            gs[tile_rows(tile, lane), :] = gate_grad[8 * tile : 8 * tile + 8]

    decay = decay_of(par)

    def step(tile, carry):
        forward, backward = map(list, carry)
        for i in range(8):
            x = xs[pl.ds(tile * 64 + i, 8, stride=8), :]
            g = gs[pl.ds((chunk // 8 - 1 - tile) * 64 + 7 - i, 8, stride=8), :]
            forward = [a * h + x for a, h in zip(decay, forward)]
            backward = [a * p + g for a, p in zip(decay, backward)]
        return tuple(forward), tuple(backward)

    zero = tuple(jnp.zeros((8, LANES), F32) for _ in range(ORDER))
    forward, backward = lax.fori_loop(0, chunk // 8, step, (zero, zero), unroll=2)
    for away, send in zip((1, 2, 3), (send1, send2, send3)):
        ahead = where[0] + away < 4
        for m in range(0, ORDER, 2):
            pair = [jnp.where(ahead, forward[n], backward[n]) for n in (m, m + 1)]
            send[8 * m : 8 * m + 16, :] = jnp.concatenate(pair, 0).astype(BF)


def final_kernel(*refs):
    (where, proj, above, below, cot, par, got1, got2, got3, *rest) = refs
    (out, proj_grad, sums_out, signal, tails, fgrads, xs, gs, ys, bs, queries_s, keys_s, values_s, held, sums, lines_s) = rest[-16:]
    chunk = cot.shape[0]
    tiles = chunk // 8

    @pl.loop(0, 8)
    def _(lane):
        weights = tap_weights(par, lane)
        for i in range(3):
            load_signal(i, proj, above, signal.at[lane], lane)
            signal[lane, i, 8 + chunk :] = below[i, :, column(lane)].astype(F32)
        here = signal.at[lane]
        queries, keys, values = (taps(i, here, weights, 0, chunk + 8) for i in range(3))
        gated = rounded(keys * values)
        queries_s[lane] = queries
        keys_s[lane] = keys
        values_s[lane] = values
        for tile in range(tiles + 1):
            rows = slice(8 * tile, 8 * tile + 8)
            if tile < tiles:
                upstream = cot[rows, column(lane)].astype(F32)
            else:
                upstream = below[3, :, column(lane)].astype(F32)
            xs[tile_rows(tile, lane), :] = gated[rows]
            gs[tile_rows(tile, lane), :] = rounded(upstream * queries[rows])

    for group in range(0, ORDER, HALF):
        modes = range(group, group + HALF)
        rates = [jnp.exp(par[line_rows(ORDER + m), :]) for m in modes]
        decay = [jnp.exp(-r) for r in rates]
        gain = [par[line_rows(m), :] for m in modes]
        entering, leaving = [], []
        for n, m in enumerate(modes):
            whole = jnp.exp(-float(chunk) * rates[n])
            scales = [None, whole, whole * whole]
            enter, leave = jnp.zeros((8, LANES), F32), jnp.zeros((8, LANES), F32)
            for away, got in zip((1, 2, 3), (got1, got2, got3)):
                pair = got[16 * (m // 2) : 16 * (m // 2) + 16, :].astype(F32)
                state = pair[8 * (m % 2) : 8 * (m % 2) + 8]
                near = state if away == 1 else scales[away - 1] * state
                far = state if away == 3 else scales[3 - away] * state
                enter = enter + jnp.where(where[0] >= away, near, 0.0)
                leave = leave + jnp.where(where[0] < away, far, 0.0)
            entering.append(enter)
            leaving.append(leave)

        def store(ref, rows, value, group=group):
            if group:
                value = value + ref[rows, :]
            ref[rows, :] = value

        def forward(tile, carry):
            states, totals = map(list, carry)
            for i in range(8):
                rows = pl.ds(tile * 64 + i, 8, stride=8)
                x, g = xs[rows, :], gs[rows, :]
                for n in range(HALF):
                    held[tile * 8 + i, n] = states[n]
                states = [a * h + x for a, h in zip(decay, states)]
                totals = [t + g * h for t, h in zip(totals, states)]
                store(ys, rows, tree([r * h for r, h in zip(gain, states)]))
            return tuple(states), tuple(totals)

        zero = tuple(jnp.zeros((8, LANES), F32) for _ in modes)
        states, totals = lax.fori_loop(0, tiles, forward, (tuple(entering), zero), unroll=2)
        for i in range(2):
            rows = line_rows(chunk + i)
            states = [a * h + xs[rows, :] for a, h in zip(decay, states)]
            store(ys, rows, tree([r * h for r, h in zip(gain, states)]))

        def backward(step, carry):
            states, counts = map(list, carry)
            tile = tiles - 1 - step
            for i in range(7, -1, -1):
                rows = pl.ds(tile * 64 + i, 8, stride=8)
                g = gs[rows, :]
                states = [a * p + g for a, p in zip(decay, states)]
                counts = [c + p * held[tile * 8 + i, n] for n, (c, p) in enumerate(zip(counts, states))]
                store(bs, rows, tree([r * p for r, p in zip(gain, states)]))
            return tuple(states), tuple(counts)

        _, counts = lax.fori_loop(0, tiles, backward, (tuple(leaving), zero), unroll=2)
        store(bs, line_rows(chunk), tree([r * p for r, p in zip(gain, leaving)]))
        after = [(p - gs[line_rows(chunk), :]) / a for a, p in zip(decay, leaving)]
        store(bs, line_rows(chunk + 1), tree([r * p for r, p in zip(gain, after)]))
        for n, m in enumerate(modes):
            sums[line_rows(m), :] = totals[n]
            sums[line_rows(ORDER + m), :] = decay[n] * counts[n]

    two = lax.broadcasted_iota(jnp.int32, (8, LANES), 0) < 2

    @pl.loop(0, 8)
    def _(lane):
        weights = tap_weights(par, lane)
        upstream = cot[:, column(lane)].astype(F32)
        tail_up = below[3, :, column(lane)].astype(F32)
        convolved = rounded(jnp.concatenate([ys[tile_rows(t, lane), :] for t in range(tiles)], 0))
        gated_grad = rounded(jnp.concatenate([bs[tile_rows(t, lane), :] for t in range(tiles)], 0))
        tail_conv = rounded(jnp.where(two, ys[tile_rows(tiles, lane), :], 0.0))
        tail_back = rounded(jnp.where(two, bs[tile_rows(tiles, lane), :], 0.0))
        out[:, column(lane)] = (queries_s[lane, 0:chunk] * convolved).astype(BF)
        lines = []
        for i in range(3):
            if i == 0:
                grad, tail = upstream * convolved, tail_up * tail_conv
            else:
                other = values_s if i == 1 else keys_s
                grad = gated_grad * other[lane, 0:chunk]
                tail = tail_back * other[lane, chunk : chunk + 8]
            fgrads[i, 0:chunk] = grad
            fgrads[i, chunk:] = tail
            total = weights[3 * i] * grad
            for j in range(1, SHORT):
                total = total + weights[3 * i + j] * fgrads[i, j : j + chunk]
            proj_grad[i, :, column(lane)] = total.astype(BF)
            for j in range(SHORT):
                lines.append(jnp.sum(grad * signal[lane, i, 8 - j : 8 - j + chunk], axis=0, keepdims=True))
        sums[tile_rows(4, lane), :] = jnp.concatenate(lines[:8], 0)
        sums[tile_rows(5, lane), :] = jnp.concatenate([lines[8], jnp.zeros((7, LANES), F32)], 0)

    for lane in range(8):
        for q in range(SUM_ROWS // 8):
            lines_s[pl.ds(lane * 64 + q, 8, stride=8), :] = lines_of_rows(sums[tile_rows(q, lane), :])

    sums_out[...] = lines_s[...].reshape(64, 8, LANES)[:, : SUM_ROWS // 8].astype(BF)


def body(names, proj, short_weight, residue, log_decay, cotangent):
    ctx, devices, n_ctx = names
    chunk, channels = cotangent.shape[1:]
    own = residue.shape[1]
    seq = chunk * n_ctx
    n_dev = channels // own
    blocks = channels // WIDE
    runs = 2 if blocks % 2 == 0 else 1
    steps = blocks // runs
    where = lax.axis_index(ctx).astype(jnp.int32).reshape(1)

    spread = pl.pallas_call(
        spread_kernel,
        out_shape=jax.ShapeDtypeStruct((n_dev, WIRE_ROWS // 8, 8 * own), BF),
        name="spread",
    )(short_weight, residue, log_decay)
    wire = lax.all_to_all(spread, devices, 0, 0, tiled=True)

    signal = proj[0].transpose(1, 0, 2)
    upstream = cotangent[0]
    right = [(i, i + 1) for i in range(n_ctx - 1)]
    left = [(i + 1, i) for i in range(n_ctx - 1)]
    above = lax.ppermute(signal[:, chunk - 8 :], ctx, right)
    below = lax.ppermute(jnp.concatenate([signal[:, :8], upstream[None, :8]], 0), ctx, left)

    def shape(dims, kind):
        return jax.ShapeDtypeStruct(dims, kind)

    scalar = pl.BlockSpec(memory_space=pltpu.SMEM)
    anywhere = pl.BlockSpec(memory_space=pl.ANY)
    vmem = lambda *dims: pltpu.VMEM(dims, F32)
    params = pltpu.CompilerParams(vmem_limit_bytes=32 * 1024 * 1024)

    def specs(run):
        def wide(*dims):
            lead = len(dims)
            return pl.BlockSpec(dims + (WIDE,), lambda i: (0,) * lead + (i + run * steps,))

        def rows(count):
            return pl.BlockSpec((WIDE // own, count // 8, 8 * own), lambda i: (i + run * steps, 0, 0))

        def whole(count):
            return pl.BlockSpec((None, count, LANES), lambda i: (i, 0, 0))

        return wide, rows, whole

    pars, gots = [], []
    for run in range(runs):
        wide, rows, whole = specs(run)
        par, *sent = pl.pallas_call(
            state_kernel,
            grid=(steps,),
            in_specs=[scalar, wide(3, chunk), wide(3, 8), wide(chunk), rows(WIRE_ROWS)],
            out_specs=[whole(8 * PAR_ROWS)] + [whole(8 * ORDER)] * 3,
            out_shape=[shape((steps, 8 * PAR_ROWS, LANES), F32)]
            + [shape((steps, 8 * ORDER, LANES), BF)] * 3,
            scratch_shapes=[
                vmem(3, chunk + 8, LANES), vmem(chunk * 8, LANES), vmem(chunk * 8, LANES), vmem(512, LANES),
            ],
            compiler_params=params,
            cost_estimate=pl.CostEstimate(flops=4 * 10**9, bytes_accessed=4 * 10**6, transcendentals=0),
            name="states",
        )(where, signal, above, upstream, wire)
        pars.append(par)
        gots.append(
            [
                lax.ppermute(values, ctx, [(i, (i + k) % n_ctx) for i in range(n_ctx)])
                for k, values in zip((1, 2, 3), sent)
            ]
        )

    results = [
        shape((chunk, channels), BF),
        shape((3, chunk, channels), BF),
        shape((n_dev, SUM_ROWS // 8, 8 * own), BF),
    ]
    made = []
    longer = chunk + 8
    for run in range(runs):
        wide, rows, whole = specs(run)
        made = pl.pallas_call(
            final_kernel,
            grid=(steps,),
            in_specs=[scalar, wide(3, chunk), wide(3, 8), wide(4, 8), wide(chunk), whole(8 * PAR_ROWS)]
            + [whole(8 * ORDER)] * 3
            + [anywhere] * len(made),
            out_specs=[wide(chunk), wide(3, chunk), rows(SUM_ROWS)],
            out_shape=results,
            scratch_shapes=[
                vmem(8, 3, chunk + 16, LANES), vmem(8, LANES), vmem(3, longer, LANES),
                vmem(longer * 8, LANES), vmem(longer * 8, LANES),
                vmem(longer * 8, LANES), vmem(longer * 8, LANES),
                vmem(8, longer, LANES), vmem(8, longer, LANES), vmem(8, longer, LANES),
                vmem(chunk, HALF, 8, LANES), vmem(8 * SUM_ROWS, LANES), vmem(512, LANES),
            ],
            input_output_aliases={9 + i: i for i in range(len(made))},
            compiler_params=params,
            cost_estimate=pl.CostEstimate(flops=8 * 10**9, bytes_accessed=8 * 10**6, transcendentals=0),
            name="final",
        )(where, signal, above, below, upstream, pars[run], *gots[run], *made)
    out, proj_grad, parts = made

    arrived = lax.all_to_all(parts, devices, 0, 0, tiled=True)
    tap_grad, residue_grad, decay_grad = pl.pallas_call(
        functools.partial(collect_kernel, 1.0 / seq),
        out_shape=[shape((3, SHORT, own), F32), shape((ORDER, own), F32), shape((ORDER, own), F32)],
        name="collect",
    )(arrived, residue, log_decay)
    return (
        out[None],
        proj_grad.transpose(1, 0, 2)[None],
        tap_grad,
        residue_grad,
        decay_grad,
    )


def solution(mesh):
    both = ("ctx", "zero")
    specs = (
        P("zero", "ctx", None, None),
        P(None, None, both),
        P(None, both),
        P(None, both),
        P("zero", "ctx", None),
    )
    out_specs = (specs[4], specs[0], specs[1], specs[2], specs[2])
    names = ("ctx", both, mesh.shape["ctx"])
    return jax.shard_map(
        functools.partial(body, names), mesh=mesh, in_specs=specs, out_specs=out_specs, check_vma=False
    )
```

```python
import functools

import jax
import jax.numpy as jnp
from jax import lax
from jax.experimental import pallas as pl
from jax.experimental.pallas import tpu as pltpu
from jax.sharding import PartitionSpec as P

SHORT = 3
ORDER = 16
LANES = 128
WIDE = 8 * LANES
WIRE = 16
WIRE_ROWS = 64
SUM_ROWS = 48
PAR_ROWS = 48
RATE_CENTRE = -5.4
HALF = ORDER // 2
BF = jnp.bfloat16
F32 = jnp.float32


def tree(parts):
    parts = list(parts)
    while len(parts) > 1:
        parts = [a + b for a, b in zip(parts[::2], parts[1::2])]
    return parts[0]


def rounded(values):
    return values.astype(BF).astype(F32)


def turn_rows(tile, forward):
    if forward:
        return pltpu.roll(tile, 0, 1, stride=WIRE, stride_axis=0)
    row = lax.broadcasted_iota(jnp.int32, (8, LANES), 0)
    place = lax.broadcasted_iota(jnp.int32, (8, LANES), 1)
    return jnp.take_along_axis(tile, (place + WIRE * row) % LANES, axis=1)


def turn_columns(tile, forward):
    column = lax.broadcasted_iota(jnp.int32, (8, LANES), 1) // WIRE
    for bit in (1, 2, 4):
        tile = jnp.where((column & bit) != 0, pltpu.roll(tile, bit if forward else 8 - bit, 0), tile)
    return tile


def rows_of_lines(tile):
    return turn_rows(turn_columns(turn_rows(tile, True), False), True)


def lines_of_rows(tile):
    return turn_rows(turn_columns(turn_rows(tile, False), True), False)


def wire_order(rows):
    return jnp.concatenate([rows[(8 - b) % 8 : (8 - b) % 8 + 1] for b in range(8)], 0)


def tile_rows(tile, lane):
    start = (tile * 8 + lane) * 8
    return pl.ds(start if isinstance(start, int) else pl.multiple_of(start, 8), 8)


def line_rows(row):
    return pl.ds((row // 8) * 64 + row % 8, 8, stride=8)


def tap_weights(par, lane):
    first = par[tile_rows(4, lane), :]
    last = par[tile_rows(5, lane), :]
    return [first[i : i + 1] for i in range(8)] + [last[0:1]]


def column(lane):
    return pl.ds(pl.multiple_of(lane * LANES, LANES), LANES)


def load_signal(which, proj, above, signal, lane):
    rows = proj.shape[1]
    signal[which, 6:8] = above[which, :, column(lane)].astype(F32)
    signal[which, 8 : 8 + rows] = proj[which, :, column(lane)].astype(F32)


def taps(which, signal, weights, start, rows):
    return tree(
        [weights[3 * which + j] * signal[which, 8 + start - j : 8 + start - j + rows] for j in range(2)]
    ) + weights[3 * which + 2] * signal[which, 6 + start : 6 + start + rows]


def padded(rows):
    return jnp.concatenate([rows.astype(F32), jnp.zeros((6, rows.shape[1]), F32)], 0)


def decay_of(par):
    return [jnp.exp(-jnp.exp(par[line_rows(ORDER + m), :])) for m in range(ORDER)]


def flat_row(rows):
    padded = jnp.concatenate([wire_order(rows), jnp.zeros((8, LANES - WIRE), F32)], 1)
    return jnp.sum(turn_rows(padded, True), axis=0, keepdims=True)


def spread_kernel(short_weight, residue, log_decay, out):
    weights = jnp.concatenate([short_weight[i] for i in range(3)], 0)
    rates = log_decay[...] - RATE_CENTRE
    rates_high, weights_high = rounded(rates), rounded(weights)
    rates_low, weights_low = rates - rates_high, weights - weights_high
    tiles = [
        rates_high[:8], rates_high[8:], rates_low[:8],
        jnp.concatenate([rates_low[8:14], weights_high[8:], weights_low[8:]], 0),
        residue[:8], residue[8:], weights_high[:8], weights_low[:8],
    ]
    rows = jnp.concatenate([flat_row(tile) for tile in tiles], 0)
    out[...] = jnp.broadcast_to(rows[None], out.shape).astype(BF)


def collect_kernel(scale, arrived, residue, log_decay, tap_grad, residue_grad, decay_grad):
    total = jnp.sum(arrived[...].astype(F32), axis=0) * scale
    tiles = [
        wire_order(turn_rows(jnp.broadcast_to(total[q : q + 1], (8, LANES)), False)[:, :WIRE])
        for q in range(SUM_ROWS // 8)
    ]
    residue_grad[...] = jnp.concatenate(tiles[0:2], 0)
    decay_grad[...] = -residue[...] * jnp.exp(log_decay[...]) * jnp.concatenate(tiles[2:4], 0)
    lines = jnp.concatenate(tiles[4:6], 0)
    for i in range(3):
        tap_grad[i] = lines[3 * i : 3 * i + 3]


def by_core(core, own, other):
    return jnp.where(core == 0, own, other), jnp.where(core == 0, other, own)


def state_kernel(where, proj, above, cot, wire, wire_pair, par, send1, send2, send3, signal, xs, gs, wires):
    chunk = cot.shape[0]
    both = by_core(where[1], wire[...].astype(F32), wire_pair[...].astype(F32))
    wires[...] = jnp.stack(both, axis=1).reshape(wires.shape)
    early = lax.broadcasted_iota(jnp.int32, (8, LANES), 0) < 6

    for lane in range(8):
        parts = [rows_of_lines(wires[pl.ds(lane * 64 + q, 8, stride=8), :]) for q in range(8)]
        par[tile_rows(0, lane), :] = parts[4]
        par[tile_rows(1, lane), :] = parts[5]
        par[tile_rows(2, lane), :] = parts[0] + parts[2] + RATE_CENTRE
        par[tile_rows(3, lane), :] = parts[1] + jnp.where(early, parts[3], 0.0) + RATE_CENTRE
        par[tile_rows(4, lane), :] = parts[6] + parts[7]
        par[tile_rows(5, lane), :] = jnp.broadcast_to(parts[3][6:7] + parts[3][7:8], (8, LANES))

    @pl.loop(0, 8, unroll=2)
    def _(lane):
        weights = tap_weights(par, lane)
        for i in range(3):
            load_signal(i, proj, above, signal, lane)
        queries, keys, values = (taps(i, signal, weights, 0, chunk) for i in range(3))
        gated = rounded(keys * values)
        gate_grad = rounded(cot[:, column(lane)].astype(F32) * queries)
        for tile in range(chunk // 8):
            xs[tile_rows(tile, lane), :] = gated[8 * tile : 8 * tile + 8]
            gs[tile_rows(tile, lane), :] = gate_grad[8 * tile : 8 * tile + 8]

    decay = decay_of(par)

    def step(tile, carry):
        forward, backward = map(list, carry)
        for i in range(8):
            x = xs[pl.ds(tile * 64 + i, 8, stride=8), :]
            g = gs[pl.ds((chunk // 8 - 1 - tile) * 64 + 7 - i, 8, stride=8), :]
            forward = [a * h + x for a, h in zip(decay, forward)]
            backward = [a * p + g for a, p in zip(decay, backward)]
        return tuple(forward), tuple(backward)

    zero = tuple(jnp.zeros((8, LANES), F32) for _ in range(ORDER))
    forward, backward = lax.fori_loop(0, chunk // 8, step, (zero, zero), unroll=2)
    for away, send in zip((1, 2, 3), (send1, send2, send3)):
        ahead = where[0] + away < 4
        for m in range(0, ORDER, 2):
            pair = [jnp.where(ahead, forward[n], backward[n]) for n in (m, m + 1)]
            send[8 * m : 8 * m + 16, :] = jnp.concatenate(pair, 0).astype(BF)


def final_kernel(*refs):
    (where, proj, above, below, cot, par, got1, got2, got3, *rest) = refs
    (out, proj_grad, sums_own, sums_pair, signal, tails, fgrads, xs, gs, ys, bs, queries_s, keys_s, values_s, held, sums, lines_s) = rest[-17:]
    chunk = cot.shape[0]
    tiles = chunk // 8

    @pl.loop(0, 8, unroll=2)
    def _(lane):
        weights = tap_weights(par, lane)
        for i in range(3):
            load_signal(i, proj, above, signal.at[lane], lane)
            signal[lane, i, 8 + chunk :] = padded(below[i, :, column(lane)])
        here = signal.at[lane]
        queries, keys, values = (taps(i, here, weights, 0, chunk + 8) for i in range(3))
        gated = rounded(keys * values)
        queries_s[lane] = queries
        keys_s[lane] = keys
        values_s[lane] = values
        for tile in range(tiles + 1):
            rows = slice(8 * tile, 8 * tile + 8)
            if tile < tiles:
                upstream = cot[rows, column(lane)].astype(F32)
            else:
                upstream = padded(below[3, :, column(lane)])
            xs[tile_rows(tile, lane), :] = gated[rows]
            gs[tile_rows(tile, lane), :] = rounded(upstream * queries[rows])

    for group in range(0, ORDER, HALF):
        modes = range(group, group + HALF)
        rates = [jnp.exp(par[line_rows(ORDER + m), :]) for m in modes]
        decay = [jnp.exp(-r) for r in rates]
        gain = [par[line_rows(m), :] for m in modes]
        entering, leaving = [], []
        for n, m in enumerate(modes):
            whole = jnp.exp(-float(chunk) * rates[n])
            scales = [None, whole, whole * whole]
            enter, leave = jnp.zeros((8, LANES), F32), jnp.zeros((8, LANES), F32)
            for away, got in zip((1, 2, 3), (got1, got2, got3)):
                pair = got[16 * (m // 2) : 16 * (m // 2) + 16, :].astype(F32)
                state = pair[8 * (m % 2) : 8 * (m % 2) + 8]
                near = state if away == 1 else scales[away - 1] * state
                far = state if away == 3 else scales[3 - away] * state
                enter = enter + jnp.where(where[0] >= away, near, 0.0)
                leave = leave + jnp.where(where[0] < away, far, 0.0)
            entering.append(enter)
            leaving.append(leave)

        def store(ref, rows, value, group=group):
            if group:
                value = value + ref[rows, :]
            ref[rows, :] = value

        def forward(tile, carry):
            states, totals = map(list, carry)
            for i in range(8):
                rows = pl.ds(tile * 64 + i, 8, stride=8)
                x, g = xs[rows, :], gs[rows, :]
                for n in range(HALF):
                    held[tile * 8 + i, n] = states[n]
                states = [a * h + x for a, h in zip(decay, states)]
                totals = [t + g * h for t, h in zip(totals, states)]
                store(ys, rows, tree([r * h for r, h in zip(gain, states)]))
            return tuple(states), tuple(totals)

        zero = tuple(jnp.zeros((8, LANES), F32) for _ in modes)
        states, totals = lax.fori_loop(0, tiles, forward, (tuple(entering), zero), unroll=2)
        for i in range(2):
            rows = line_rows(chunk + i)
            states = [a * h + xs[rows, :] for a, h in zip(decay, states)]
            store(ys, rows, tree([r * h for r, h in zip(gain, states)]))

        def backward(step, carry):
            states, counts = map(list, carry)
            tile = tiles - 1 - step
            for i in range(7, -1, -1):
                rows = pl.ds(tile * 64 + i, 8, stride=8)
                g = gs[rows, :]
                states = [a * p + g for a, p in zip(decay, states)]
                counts = [c + p * held[tile * 8 + i, n] for n, (c, p) in enumerate(zip(counts, states))]
                store(bs, rows, tree([r * p for r, p in zip(gain, states)]))
            return tuple(states), tuple(counts)

        _, counts = lax.fori_loop(0, tiles, backward, (tuple(leaving), zero), unroll=2)
        store(bs, line_rows(chunk), tree([r * p for r, p in zip(gain, leaving)]))
        after = [(p - gs[line_rows(chunk), :]) / a for a, p in zip(decay, leaving)]
        store(bs, line_rows(chunk + 1), tree([r * p for r, p in zip(gain, after)]))
        for n, m in enumerate(modes):
            sums[line_rows(m), :] = totals[n]
            sums[line_rows(ORDER + m), :] = decay[n] * counts[n]

    two = lax.broadcasted_iota(jnp.int32, (8, LANES), 0) < 2

    @pl.loop(0, 8, unroll=2)
    def _(lane):
        weights = tap_weights(par, lane)
        upstream = cot[:, column(lane)].astype(F32)
        tail_up = padded(below[3, :, column(lane)])
        convolved = rounded(jnp.concatenate([ys[tile_rows(t, lane), :] for t in range(tiles)], 0))
        gated_grad = rounded(jnp.concatenate([bs[tile_rows(t, lane), :] for t in range(tiles)], 0))
        tail_conv = rounded(jnp.where(two, ys[tile_rows(tiles, lane), :], 0.0))
        tail_back = rounded(jnp.where(two, bs[tile_rows(tiles, lane), :], 0.0))
        out[:, column(lane)] = (queries_s[lane, 0:chunk] * convolved).astype(BF)
        lines = []
        for i in range(3):
            if i == 0:
                grad, tail = upstream * convolved, tail_up * tail_conv
            else:
                other = values_s if i == 1 else keys_s
                grad = gated_grad * other[lane, 0:chunk]
                tail = tail_back * other[lane, chunk : chunk + 8]
            fgrads[i, 0:chunk] = grad
            fgrads[i, chunk:] = tail
            total = weights[3 * i] * grad
            for j in range(1, SHORT):
                total = total + weights[3 * i + j] * fgrads[i, j : j + chunk]
            proj_grad[i, :, column(lane)] = total.astype(BF)
            for j in range(SHORT):
                lines.append(jnp.sum(grad * signal[lane, i, 8 - j : 8 - j + chunk], axis=0, keepdims=True))
        sums[tile_rows(4, lane), :] = jnp.concatenate(lines[:8], 0)
        sums[tile_rows(5, lane), :] = jnp.concatenate([lines[8], jnp.zeros((7, LANES), F32)], 0)

    for lane in range(8):
        for q in range(SUM_ROWS // 8):
            lines_s[pl.ds(lane * 64 + q, 8, stride=8), :] = lines_of_rows(sums[tile_rows(q, lane), :])

    lines = lines_s[...].reshape(32, 2, 8, LANES)[:, :, : SUM_ROWS // 8].astype(BF)
    sums_own[...], sums_pair[...] = by_core(where[1], lines[:, 0], lines[:, 1])


def body(names, proj, short_weight, residue, log_decay, cotangent):
    ctx, devices, n_ctx = names
    chunk, channels = cotangent.shape[1:]
    own = residue.shape[1]
    seq = chunk * n_ctx
    n_dev = channels // own
    blocks = channels // WIDE
    runs = 2 if blocks % 2 == 0 else 1
    steps = blocks // runs
    zero = devices[1]
    n_zero = n_dev // n_ctx
    where = jnp.stack([lax.axis_index(ctx), lax.axis_index(zero) % 2]).astype(jnp.int32)
    cores = [[i for i in range(n_dev) if i % 2 == c] for c in range(2)]

    def from_all(values):
        return lax.all_to_all(values, devices, 0, 0, tiled=True, axis_index_groups=cores)

    def from_pair(values):
        return lax.ppermute(values, zero, [(i, i ^ 1) for i in range(n_zero)])


    spread = pl.pallas_call(
        spread_kernel,
        out_shape=jax.ShapeDtypeStruct((n_dev // 2, WIRE_ROWS // 8, 8 * own), BF),
        name="spread",
    )(short_weight, residue, log_decay)
    wire = from_all(spread)
    wire_pair = from_pair(wire)

    signal = proj[0].transpose(1, 0, 2)
    upstream = cotangent[0]
    right = [(i, i + 1) for i in range(n_ctx - 1)]
    left = [(i + 1, i) for i in range(n_ctx - 1)]
    above = lax.ppermute(signal[:, chunk - 2 :], ctx, right)
    below = lax.ppermute(jnp.concatenate([signal[:, :2], upstream[None, :2]], 0), ctx, left)

    def shape(dims, kind):
        return jax.ShapeDtypeStruct(dims, kind)

    scalar = pl.BlockSpec(memory_space=pltpu.SMEM)
    anywhere = pl.BlockSpec(memory_space=pl.ANY)
    vmem = lambda *dims: pltpu.VMEM(dims, F32)
    params = pltpu.CompilerParams(vmem_limit_bytes=32 * 1024 * 1024)

    def specs(run):
        def wide(*dims):
            lead = len(dims)
            return pl.BlockSpec(dims + (WIDE,), lambda i: (0,) * lead + (i + run * steps,))

        def rows(count):
            return pl.BlockSpec((WIDE // own // 2, count // 8, 8 * own), lambda i: (i + run * steps, 0, 0))

        def whole(count):
            return pl.BlockSpec((None, count, LANES), lambda i: (i, 0, 0))

        return wide, rows, whole

    pars, gots = [], []
    for run in range(runs):
        wide, rows, whole = specs(run)
        par, *sent = pl.pallas_call(
            state_kernel,
            grid=(steps,),
            in_specs=[scalar, wide(3, chunk), wide(3, 2), wide(chunk), rows(WIRE_ROWS), rows(WIRE_ROWS)],
            out_specs=[whole(8 * PAR_ROWS)] + [whole(8 * ORDER)] * 3,
            out_shape=[shape((steps, 8 * PAR_ROWS, LANES), F32)]
            + [shape((steps, 8 * ORDER, LANES), BF)] * 3,
            scratch_shapes=[
                vmem(3, chunk + 8, LANES), vmem(chunk * 8, LANES), vmem(chunk * 8, LANES), vmem(512, LANES),
            ],
            compiler_params=params,
            cost_estimate=pl.CostEstimate(flops=4 * 10**9, bytes_accessed=4 * 10**6, transcendentals=0),
            name="states",
        )(where, signal, above, upstream, wire, wire_pair)
        pars.append(par)
        gots.append(
            [
                lax.ppermute(values, ctx, [(i, (i + k) % n_ctx) for i in range(n_ctx)])
                for k, values in zip((1, 2, 3), sent)
            ]
        )

    results = [
        shape((chunk, channels), BF),
        shape((3, chunk, channels), BF),
    ] + [shape((n_dev // 2, SUM_ROWS // 8, 8 * own), BF)] * 2
    made = []
    longer = chunk + 8
    for run in range(runs):
        wide, rows, whole = specs(run)
        made = pl.pallas_call(
            final_kernel,
            grid=(steps,),
            in_specs=[scalar, wide(3, chunk), wide(3, 2), wide(4, 2), wide(chunk), whole(8 * PAR_ROWS)]
            + [whole(8 * ORDER)] * 3
            + [anywhere] * len(made),
            out_specs=[wide(chunk), wide(3, chunk), rows(SUM_ROWS), rows(SUM_ROWS)],
            out_shape=results,
            scratch_shapes=[
                vmem(8, 3, chunk + 16, LANES), vmem(8, LANES), vmem(3, longer, LANES),
                vmem(longer * 8, LANES), vmem(longer * 8, LANES),
                vmem(longer * 8, LANES), vmem(longer * 8, LANES),
                vmem(8, longer, LANES), vmem(8, longer, LANES), vmem(8, longer, LANES),
                vmem(chunk, HALF, 8, LANES), vmem(8 * SUM_ROWS, LANES), vmem(512, LANES),
            ],
            input_output_aliases={9 + i: i for i in range(len(made))},
            compiler_params=params,
            cost_estimate=pl.CostEstimate(flops=8 * 10**9, bytes_accessed=8 * 10**6, transcendentals=0),
            name="final",
        )(where, signal, above, below, upstream, pars[run], *gots[run], *made)
    out, proj_grad, parts_own, parts_pair = made

    pair_sum = parts_own.astype(F32) + from_pair(parts_pair).astype(F32)
    arrived = from_all(pair_sum.astype(BF))
    tap_grad, residue_grad, decay_grad = pl.pallas_call(
        functools.partial(collect_kernel, 1.0 / seq),
        out_shape=[shape((3, SHORT, own), F32), shape((ORDER, own), F32), shape((ORDER, own), F32)],
        name="collect",
    )(arrived, residue, log_decay)
    return (
        out[None],
        proj_grad.transpose(1, 0, 2)[None],
        tap_grad,
        residue_grad,
        decay_grad,
    )


def solution(mesh):
    both = ("ctx", "zero")
    specs = (
        P("zero", "ctx", None, None),
        P(None, None, both),
        P(None, both),
        P(None, both),
        P("zero", "ctx", None),
    )
    out_specs = (specs[4], specs[0], specs[1], specs[2], specs[2])
    names = ("ctx", both, mesh.shape["ctx"])
    return jax.shard_map(
        functools.partial(body, names), mesh=mesh, in_specs=specs, out_specs=out_specs, check_vma=False
    )
```

```python
import functools

import jax
import jax.numpy as jnp
from jax import lax
from jax.experimental import pallas as pl
from jax.experimental.pallas import tpu as pltpu
from jax.sharding import PartitionSpec as P

SHORT = 3
ORDER = 16
LANES = 128
WIDE = 8 * LANES
WIRE = 16
WIRE_ROWS = 64
SUM_ROWS = 48
PAR_ROWS = 48
RATE_CENTRE = -5.4
HALF = ORDER // 2
BF = jnp.bfloat16
F32 = jnp.float32


def tree(parts):
    parts = list(parts)
    while len(parts) > 1:
        parts = [a + b for a, b in zip(parts[::2], parts[1::2])]
    return parts[0]


def rounded(values):
    return values.astype(BF).astype(F32)


def turn_rows(tile, forward):
    if forward:
        return pltpu.roll(tile, 0, 1, stride=WIRE, stride_axis=0)
    row = lax.broadcasted_iota(jnp.int32, (8, LANES), 0)
    place = lax.broadcasted_iota(jnp.int32, (8, LANES), 1)
    return jnp.take_along_axis(tile, (place + WIRE * row) % LANES, axis=1)


def turn_columns(tile, forward):
    column = lax.broadcasted_iota(jnp.int32, (8, LANES), 1) // WIRE
    for bit in (1, 2, 4):
        tile = jnp.where((column & bit) != 0, pltpu.roll(tile, bit if forward else 8 - bit, 0), tile)
    return tile


def rows_of_lines(tile):
    return turn_rows(turn_columns(turn_rows(tile, True), False), True)


def lines_of_rows(tile):
    return turn_rows(turn_columns(turn_rows(tile, False), True), False)


def wire_order(rows):
    return jnp.concatenate([rows[(8 - b) % 8 : (8 - b) % 8 + 1] for b in range(8)], 0)


def tile_rows(tile, lane):
    start = (tile * 8 + lane) * 8
    return pl.ds(start if isinstance(start, int) else pl.multiple_of(start, 8), 8)


def line_rows(row):
    return pl.ds((row // 8) * 64 + row % 8, 8, stride=8)


def tap_weights(par, lane):
    first = par[tile_rows(4, lane), :]
    last = par[tile_rows(5, lane), :]
    return [first[i : i + 1] for i in range(8)] + [last[0:1]]


def column(lane):
    return pl.ds(pl.multiple_of(lane * LANES, LANES), LANES)


def load_signal(which, proj, above, signal, lane):
    rows = proj.shape[1]
    signal[which, 6:8] = above[which, :, column(lane)].astype(F32)
    signal[which, 8 : 8 + rows] = proj[which, :, column(lane)].astype(F32)


def taps(which, signal, weights, start, rows):
    return tree(
        [weights[3 * which + j] * signal[which, 8 + start - j : 8 + start - j + rows] for j in range(2)]
    ) + weights[3 * which + 2] * signal[which, 6 + start : 6 + start + rows]


def head_rows(parts):
    row = lax.broadcasted_iota(jnp.int32, (8, LANES), 0)
    made = parts[0]
    for i in range(1, 4):
        made = jnp.where(row >= 2 * i, pltpu.roll(parts[i], 2 * i, 0), made)
    return made


def padded(tails, lane, which):
    rows = tails[pl.ds(pl.multiple_of(lane * 8, 8), 8), :][2 * which : 2 * which + 2]
    return jnp.concatenate([rows, jnp.zeros((6, LANES), F32)], 0)


def decay_of(par):
    return [jnp.exp(-jnp.exp(par[line_rows(ORDER + m), :])) for m in range(ORDER)]


def flat_row(rows):
    padded = jnp.concatenate([wire_order(rows), jnp.zeros((8, LANES - WIRE), F32)], 1)
    return jnp.sum(turn_rows(padded, True), axis=0, keepdims=True)


def spread_kernel(short_weight, residue, log_decay, out):
    weights = jnp.concatenate([short_weight[i] for i in range(3)], 0)
    rates = log_decay[...] - RATE_CENTRE
    rates_high, weights_high = rounded(rates), rounded(weights)
    rates_low, weights_low = rates - rates_high, weights - weights_high
    tiles = [
        rates_high[:8], rates_high[8:], rates_low[:8],
        jnp.concatenate([rates_low[8:14], weights_high[8:], weights_low[8:]], 0),
        residue[:8], residue[8:], weights_high[:8], weights_low[:8],
    ]
    rows = jnp.concatenate([flat_row(tile) for tile in tiles], 0)
    out[...] = jnp.broadcast_to(rows[None], out.shape).astype(BF)


def collect_kernel(scale, arrived, residue, log_decay, tap_grad, residue_grad, decay_grad):
    total = jnp.sum(arrived[...].astype(F32), axis=0) * scale
    tiles = [
        wire_order(turn_rows(jnp.broadcast_to(total[q : q + 1], (8, LANES)), False)[:, :WIRE])
        for q in range(SUM_ROWS // 8)
    ]
    residue_grad[...] = jnp.concatenate(tiles[0:2], 0)
    decay_grad[...] = -residue[...] * jnp.exp(log_decay[...]) * jnp.concatenate(tiles[2:4], 0)
    lines = jnp.concatenate(tiles[4:6], 0)
    for i in range(3):
        tap_grad[i] = lines[3 * i : 3 * i + 3]


def by_core(core, own, other):
    return jnp.where(core == 0, own, other), jnp.where(core == 0, other, own)


def state_kernel(where, proj, above, cot, wire, wire_pair, par, send1, send2, send3, signal, xs, gs, wires, halo):
    chunk = cot.shape[0]
    both = by_core(where[1], wire[...].astype(F32), wire_pair[...].astype(F32))
    wires[...] = jnp.stack(both, axis=1).reshape(wires.shape)
    early = lax.broadcasted_iota(jnp.int32, (8, LANES), 0) < 6

    for lane in range(8):
        parts = [rows_of_lines(wires[pl.ds(lane * 64 + q, 8, stride=8), :]) for q in range(8)]
        par[tile_rows(0, lane), :] = parts[4]
        par[tile_rows(1, lane), :] = parts[5]
        par[tile_rows(2, lane), :] = parts[0] + parts[2] + RATE_CENTRE
        par[tile_rows(3, lane), :] = parts[1] + jnp.where(early, parts[3], 0.0) + RATE_CENTRE
        par[tile_rows(4, lane), :] = parts[6] + parts[7]
        par[tile_rows(5, lane), :] = jnp.broadcast_to(parts[3][6:7] + parts[3][7:8], (8, LANES))

    @pl.loop(0, 8, unroll=2)
    def _(lane):
        weights = tap_weights(par, lane)
        for i in range(3):
            load_signal(i, proj, above, signal, lane)
        queries, keys, values = (taps(i, signal, weights, 0, chunk) for i in range(3))
        gated = rounded(keys * values)
        upstream = cot[:, column(lane)].astype(F32)
        gate_grad = rounded(upstream * queries)
        first = [signal[i, 8:16] for i in range(3)] + [upstream[0:8]]
        halo[pl.ds(pl.multiple_of(lane * 8, 8), 8), :] = head_rows(first)
        for tile in range(chunk // 8):
            xs[tile_rows(tile, lane), :] = gated[8 * tile : 8 * tile + 8]
            gs[tile_rows(tile, lane), :] = gate_grad[8 * tile : 8 * tile + 8]

    decay = decay_of(par)

    def step(tile, carry):
        forward, backward = map(list, carry)
        for i in range(8):
            x = xs[pl.ds(tile * 64 + i, 8, stride=8), :]
            g = gs[pl.ds((chunk // 8 - 1 - tile) * 64 + 7 - i, 8, stride=8), :]
            forward = [a * h + x for a, h in zip(decay, forward)]
            backward = [a * p + g for a, p in zip(decay, backward)]
        return tuple(forward), tuple(backward)

    zero = tuple(jnp.zeros((8, LANES), F32) for _ in range(ORDER))
    forward, backward = lax.fori_loop(0, chunk // 8, step, (zero, zero), unroll=2)
    send3[8 * ORDER :, :] = halo[...].astype(BF)
    for away, send in zip((1, 2, 3), (send1, send2, send3)):
        ahead = where[0] + away < 4
        for m in range(0, ORDER, 2):
            pair = [jnp.where(ahead, forward[n], backward[n]) for n in (m, m + 1)]
            send[8 * m : 8 * m + 16, :] = jnp.concatenate(pair, 0).astype(BF)


def final_kernel(*refs):
    (where, proj, above, cot, par, got1, got2, got3, *rest) = refs
    (out, proj_grad, sums_own, sums_pair, signal, tails, fgrads, xs, gs, ys, bs, queries_s, keys_s, values_s, held, sums, lines_s) = rest[-17:]
    chunk = cot.shape[0]
    tiles = chunk // 8
    follows = jnp.where(where[0] < 3, 1.0, 0.0)
    tails[...] = got3[8 * ORDER :, :].astype(F32) * follows

    @pl.loop(0, 8, unroll=2)
    def _(lane):
        weights = tap_weights(par, lane)
        for i in range(3):
            load_signal(i, proj, above, signal.at[lane], lane)
            signal[lane, i, 8 + chunk :] = padded(tails, lane, i)
        here = signal.at[lane]
        queries, keys, values = (taps(i, here, weights, 0, chunk + 8) for i in range(3))
        gated = rounded(keys * values)
        queries_s[lane] = queries
        keys_s[lane] = keys
        values_s[lane] = values
        for tile in range(tiles + 1):
            rows = slice(8 * tile, 8 * tile + 8)
            if tile < tiles:
                upstream = cot[rows, column(lane)].astype(F32)
            else:
                upstream = padded(tails, lane, 3)
            xs[tile_rows(tile, lane), :] = gated[rows]
            gs[tile_rows(tile, lane), :] = rounded(upstream * queries[rows])

    for group in range(0, ORDER, HALF):
        modes = range(group, group + HALF)
        rates = [jnp.exp(par[line_rows(ORDER + m), :]) for m in modes]
        decay = [jnp.exp(-r) for r in rates]
        gain = [par[line_rows(m), :] for m in modes]
        entering, leaving = [], []
        for n, m in enumerate(modes):
            whole = jnp.exp(-float(chunk) * rates[n])
            scales = [None, whole, whole * whole]
            enter, leave = jnp.zeros((8, LANES), F32), jnp.zeros((8, LANES), F32)
            for away, got in zip((1, 2, 3), (got1, got2, got3)):
                pair = got[16 * (m // 2) : 16 * (m // 2) + 16, :].astype(F32)
                state = pair[8 * (m % 2) : 8 * (m % 2) + 8]
                near = state if away == 1 else scales[away - 1] * state
                far = state if away == 3 else scales[3 - away] * state
                enter = enter + jnp.where(where[0] >= away, near, 0.0)
                leave = leave + jnp.where(where[0] < away, far, 0.0)
            entering.append(enter)
            leaving.append(leave)

        def store(ref, rows, value, group=group):
            if group:
                value = value + ref[rows, :]
            ref[rows, :] = value

        def forward(tile, carry):
            states, totals = map(list, carry)
            for i in range(8):
                rows = pl.ds(tile * 64 + i, 8, stride=8)
                x, g = xs[rows, :], gs[rows, :]
                for n in range(HALF):
                    held[tile * 8 + i, n] = states[n]
                states = [a * h + x for a, h in zip(decay, states)]
                totals = [t + g * h for t, h in zip(totals, states)]
                store(ys, rows, tree([r * h for r, h in zip(gain, states)]))
            return tuple(states), tuple(totals)

        zero = tuple(jnp.zeros((8, LANES), F32) for _ in modes)
        states, totals = lax.fori_loop(0, tiles, forward, (tuple(entering), zero), unroll=2)
        for i in range(2):
            rows = line_rows(chunk + i)
            states = [a * h + xs[rows, :] for a, h in zip(decay, states)]
            store(ys, rows, tree([r * h for r, h in zip(gain, states)]))

        def backward(step, carry):
            states, counts = map(list, carry)
            tile = tiles - 1 - step
            for i in range(7, -1, -1):
                rows = pl.ds(tile * 64 + i, 8, stride=8)
                g = gs[rows, :]
                states = [a * p + g for a, p in zip(decay, states)]
                counts = [c + p * held[tile * 8 + i, n] for n, (c, p) in enumerate(zip(counts, states))]
                store(bs, rows, tree([r * p for r, p in zip(gain, states)]))
            return tuple(states), tuple(counts)

        _, counts = lax.fori_loop(0, tiles, backward, (tuple(leaving), zero), unroll=2)
        store(bs, line_rows(chunk), tree([r * p for r, p in zip(gain, leaving)]))
        after = [(p - gs[line_rows(chunk), :]) / a for a, p in zip(decay, leaving)]
        store(bs, line_rows(chunk + 1), tree([r * p for r, p in zip(gain, after)]))
        for n, m in enumerate(modes):
            sums[line_rows(m), :] = totals[n]
            sums[line_rows(ORDER + m), :] = decay[n] * counts[n]

    two = lax.broadcasted_iota(jnp.int32, (8, LANES), 0) < 2

    @pl.loop(0, 8, unroll=2)
    def _(lane):
        weights = tap_weights(par, lane)
        upstream = cot[:, column(lane)].astype(F32)
        tail_up = padded(tails, lane, 3)
        convolved = rounded(jnp.concatenate([ys[tile_rows(t, lane), :] for t in range(tiles)], 0))
        gated_grad = rounded(jnp.concatenate([bs[tile_rows(t, lane), :] for t in range(tiles)], 0))
        tail_conv = rounded(jnp.where(two, ys[tile_rows(tiles, lane), :], 0.0))
        tail_back = rounded(jnp.where(two, bs[tile_rows(tiles, lane), :], 0.0))
        out[:, column(lane)] = (queries_s[lane, 0:chunk] * convolved).astype(BF)
        lines = []
        for i in range(3):
            if i == 0:
                grad, tail = upstream * convolved, tail_up * tail_conv
            else:
                other = values_s if i == 1 else keys_s
                grad = gated_grad * other[lane, 0:chunk]
                tail = tail_back * other[lane, chunk : chunk + 8]
            fgrads[i, 0:chunk] = grad
            fgrads[i, chunk:] = tail
            total = weights[3 * i] * grad
            for j in range(1, SHORT):
                total = total + weights[3 * i + j] * fgrads[i, j : j + chunk]
            proj_grad[i, :, column(lane)] = total.astype(BF)
            for j in range(SHORT):
                lines.append(jnp.sum(grad * signal[lane, i, 8 - j : 8 - j + chunk], axis=0, keepdims=True))
        sums[tile_rows(4, lane), :] = jnp.concatenate(lines[:8], 0)
        sums[tile_rows(5, lane), :] = jnp.concatenate([lines[8], jnp.zeros((7, LANES), F32)], 0)

    for lane in range(8):
        for q in range(SUM_ROWS // 8):
            lines_s[pl.ds(lane * 64 + q, 8, stride=8), :] = lines_of_rows(sums[tile_rows(q, lane), :])

    lines = lines_s[...].reshape(32, 2, 8, LANES)[:, :, : SUM_ROWS // 8].astype(BF)
    sums_own[...], sums_pair[...] = by_core(where[1], lines[:, 0], lines[:, 1])


def body(names, proj, short_weight, residue, log_decay, cotangent):
    ctx, devices, n_ctx = names
    chunk, channels = cotangent.shape[1:]
    own = residue.shape[1]
    seq = chunk * n_ctx
    n_dev = channels // own
    blocks = channels // WIDE
    runs = 2 if blocks % 2 == 0 else 1
    steps = blocks // runs
    zero = devices[1]
    n_zero = n_dev // n_ctx
    where = jnp.stack([lax.axis_index(ctx), lax.axis_index(zero) % 2]).astype(jnp.int32)
    cores = [[i for i in range(n_dev) if i % 2 == c] for c in range(2)]

    def from_all(values):
        return lax.all_to_all(values, devices, 0, 0, tiled=True, axis_index_groups=cores)

    def from_pair(values):
        return lax.ppermute(values, zero, [(i, i ^ 1) for i in range(n_zero)])


    spread = pl.pallas_call(
        spread_kernel,
        out_shape=jax.ShapeDtypeStruct((n_dev // 2, WIRE_ROWS // 8, 8 * own), BF),
        name="spread",
    )(short_weight, residue, log_decay)
    signal, spread = lax.optimization_barrier((proj[0].transpose(1, 0, 2), spread))
    wire = from_all(spread)

    upstream = cotangent[0]
    above = lax.ppermute(signal[:, chunk - 2 :], ctx, [(i, i + 1) for i in range(n_ctx - 1)])

    def shape(dims, kind):
        return jax.ShapeDtypeStruct(dims, kind)

    scalar = pl.BlockSpec(memory_space=pltpu.SMEM)
    anywhere = pl.BlockSpec(memory_space=pl.ANY)
    vmem = lambda *dims: pltpu.VMEM(dims, F32)
    params = pltpu.CompilerParams(vmem_limit_bytes=32 * 1024 * 1024)

    def specs(run):
        def wide(*dims):
            lead = len(dims)
            return pl.BlockSpec(dims + (WIDE,), lambda i: (0,) * lead + (i + run * steps,))

        def rows(count):
            return pl.BlockSpec((WIDE // own // 2, count // 8, 8 * own), lambda i: (i + run * steps, 0, 0))

        def whole(count):
            return pl.BlockSpec((None, count, LANES), lambda i: (i, 0, 0))

        def local(*dims):
            lead = len(dims)
            return pl.BlockSpec(dims + (WIDE,), lambda i: (0,) * lead + (i,))

        return wide, rows, whole, local

    width = steps * WIDE
    signals = [signal[:, :, run * width : run * width + width] for run in range(runs)]
    upstreams = [upstream[:, run * width : run * width + width] for run in range(runs)]

    wire, above, signals, upstreams = lax.optimization_barrier((wire, above, signals, upstreams))
    wire_pair = from_pair(wire)
    sizes = (8 * ORDER, 8 * ORDER, 8 * ORDER + 64)
    pars, gots = [], []
    for run in range(runs):
        wide, rows, whole, local = specs(run)
        par, *sent = pl.pallas_call(
            state_kernel,
            grid=(steps,),
            in_specs=[scalar, local(3, chunk), wide(3, 2), local(chunk), rows(WIRE_ROWS), rows(WIRE_ROWS)],
            out_specs=[whole(8 * PAR_ROWS)] + [whole(n) for n in sizes],
            out_shape=[shape((steps, 8 * PAR_ROWS, LANES), F32)]
            + [shape((steps, n, LANES), BF) for n in sizes],
            scratch_shapes=[
                vmem(3, chunk + 8, LANES), vmem(chunk * 8, LANES), vmem(chunk * 8, LANES), vmem(512, LANES),
                vmem(64, LANES),
            ],
            compiler_params=params,
            cost_estimate=pl.CostEstimate(flops=4 * 10**9, bytes_accessed=4 * 10**6, transcendentals=0),
            name="states",
        )(where, signals[run], above, upstreams[run], wire, wire_pair)
        pars.append(par)
        gots.append(
            [
                lax.ppermute(values, ctx, [(i, (i + k) % n_ctx) for i in range(n_ctx)])
                for k, values in zip((1, 2, 3), sent)
            ]
        )

    results = [
        shape((chunk, channels), BF),
        shape((3, chunk, channels), BF),
    ] + [shape((n_dev // 2, SUM_ROWS // 8, 8 * own), BF)] * 2
    made = []
    longer = chunk + 8
    for run in range(runs):
        wide, rows, whole, local = specs(run)
        made = pl.pallas_call(
            final_kernel,
            grid=(steps,),
            in_specs=[scalar, local(3, chunk), wide(3, 2), local(chunk), whole(8 * PAR_ROWS)]
            + [whole(n) for n in sizes]
            + [anywhere] * len(made),
            out_specs=[wide(chunk), wide(3, chunk), rows(SUM_ROWS), rows(SUM_ROWS)],
            out_shape=results,
            scratch_shapes=[
                vmem(8, 3, chunk + 16, LANES), vmem(64, LANES), vmem(3, longer, LANES),
                vmem(longer * 8, LANES), vmem(longer * 8, LANES),
                vmem(longer * 8, LANES), vmem(longer * 8, LANES),
                vmem(8, longer, LANES), vmem(8, longer, LANES), vmem(8, longer, LANES),
                vmem(chunk, HALF, 8, LANES), vmem(8 * SUM_ROWS, LANES), vmem(512, LANES),
            ],
            input_output_aliases={8 + i: i for i in range(len(made))},
            compiler_params=params,
            cost_estimate=pl.CostEstimate(flops=8 * 10**9, bytes_accessed=8 * 10**6, transcendentals=0),
            name="final",
        )(where, signals[run], above, upstreams[run], pars[run], *gots[run], *made)
    out, proj_grad, parts_own, parts_pair = made

    pair_sum = parts_own.astype(F32) + from_pair(parts_pair).astype(F32)
    arrived = from_all(pair_sum.astype(BF))
    tap_grad, residue_grad, decay_grad = pl.pallas_call(
        functools.partial(collect_kernel, 1.0 / seq),
        out_shape=[shape((3, SHORT, own), F32), shape((ORDER, own), F32), shape((ORDER, own), F32)],
        name="collect",
    )(arrived, residue, log_decay)
    return (
        out[None],
        proj_grad.transpose(1, 0, 2)[None],
        tap_grad,
        residue_grad,
        decay_grad,
    )


def solution(mesh):
    both = ("ctx", "zero")
    specs = (
        P("zero", "ctx", None, None),
        P(None, None, both),
        P(None, both),
        P(None, both),
        P("zero", "ctx", None),
    )
    out_specs = (specs[4], specs[0], specs[1], specs[2], specs[2])
    names = ("ctx", both, mesh.shape["ctx"])
    return jax.shard_map(
        functools.partial(body, names), mesh=mesh, in_specs=specs, out_specs=out_specs, check_vma=False
    )
```

```python
import functools

import jax
import jax.numpy as jnp
from jax import lax
from jax.experimental import pallas as pl
from jax.experimental.pallas import tpu as pltpu
from jax.sharding import PartitionSpec as P

SHORT = 3
ORDER = 16
LANES = 128
WIDE = 8 * LANES
WIRE = 16
WIRE_ROWS = 64
SUM_ROWS = 48
PAR_ROWS = 48
RATE_CENTRE = -5.4
HALF = ORDER // 2
BF = jnp.bfloat16
F32 = jnp.float32


def tree(parts):
    parts = list(parts)
    while len(parts) > 1:
        parts = [a + b for a, b in zip(parts[::2], parts[1::2])]
    return parts[0]


def rounded(values):
    return values.astype(BF).astype(F32)


def turn_rows(tile, forward):
    if forward:
        return pltpu.roll(tile, 0, 1, stride=WIRE, stride_axis=0)
    row = lax.broadcasted_iota(jnp.int32, (8, LANES), 0)
    place = lax.broadcasted_iota(jnp.int32, (8, LANES), 1)
    return jnp.take_along_axis(tile, (place + WIRE * row) % LANES, axis=1)


def turn_columns(tile, forward):
    column = lax.broadcasted_iota(jnp.int32, (8, LANES), 1) // WIRE
    for bit in (1, 2, 4):
        tile = jnp.where((column & bit) != 0, pltpu.roll(tile, bit if forward else 8 - bit, 0), tile)
    return tile


def rows_of_lines(tile):
    return turn_rows(turn_columns(turn_rows(tile, True), False), True)


def lines_of_rows(tile):
    return turn_rows(turn_columns(turn_rows(tile, False), True), False)


def wire_order(rows):
    return jnp.concatenate([rows[(8 - b) % 8 : (8 - b) % 8 + 1] for b in range(8)], 0)


def tile_rows(tile, lane):
    start = (tile * 8 + lane) * 8
    return pl.ds(start if isinstance(start, int) else pl.multiple_of(start, 8), 8)


def line_rows(row):
    return pl.ds((row // 8) * 64 + row % 8, 8, stride=8)


def tap_weights(par, lane):
    first = par[tile_rows(4, lane), :]
    last = par[tile_rows(5, lane), :]
    return [first[i : i + 1] for i in range(8)] + [last[0:1]]


def column(lane):
    return pl.ds(pl.multiple_of(lane * LANES, LANES), LANES)


def load_signal(which, proj, above, signal, lane):
    rows = proj.shape[1]
    signal[which, 6:8] = above[which, :, column(lane)].astype(F32)
    signal[which, 8 : 8 + rows] = proj[which, :, column(lane)].astype(F32)


def taps(which, signal, weights, start, rows):
    return tree(
        [weights[3 * which + j] * signal[which, 8 + start - j : 8 + start - j + rows] for j in range(2)]
    ) + weights[3 * which + 2] * signal[which, 6 + start : 6 + start + rows]


def head_rows(parts):
    row = lax.broadcasted_iota(jnp.int32, (8, LANES), 0)
    made = parts[0]
    for i in range(1, 4):
        made = jnp.where(row >= 2 * i, pltpu.roll(parts[i], 2 * i, 0), made)
    return made


def padded(tails, lane, which):
    rows = tails[pl.ds(pl.multiple_of(lane * 8, 8), 8), :][2 * which : 2 * which + 2]
    return jnp.concatenate([rows, jnp.zeros((6, LANES), F32)], 0)


def decay_of(par):
    return [jnp.exp(-jnp.exp(par[line_rows(ORDER + m), :])) for m in range(ORDER)]


def flat_row(rows):
    padded = jnp.concatenate([wire_order(rows), jnp.zeros((8, LANES - WIRE), F32)], 1)
    return jnp.sum(turn_rows(padded, True), axis=0, keepdims=True)


def spread_kernel(short_weight, residue, log_decay, out):
    weights = jnp.concatenate([short_weight[i] for i in range(3)], 0)
    rates = log_decay[...] - RATE_CENTRE
    rates_high, weights_high = rounded(rates), rounded(weights)
    rates_low, weights_low = rates - rates_high, weights - weights_high
    tiles = [
        rates_high[:8], rates_high[8:], rates_low[:8],
        jnp.concatenate([rates_low[8:14], weights_high[8:], weights_low[8:]], 0),
        residue[:8], residue[8:], weights_high[:8], weights_low[:8],
    ]
    rows = jnp.concatenate([flat_row(tile) for tile in tiles], 0)
    out[...] = jnp.broadcast_to(rows[None], out.shape).astype(BF)


def collect_kernel(scale, arrived, residue, log_decay, tap_grad, residue_grad, decay_grad):
    total = jnp.sum(arrived[...].astype(F32), axis=0) * scale
    tiles = [
        wire_order(turn_rows(jnp.broadcast_to(total[q : q + 1], (8, LANES)), False)[:, :WIRE])
        for q in range(SUM_ROWS // 8)
    ]
    residue_grad[...] = jnp.concatenate(tiles[0:2], 0)
    decay_grad[...] = -residue[...] * jnp.exp(log_decay[...]) * jnp.concatenate(tiles[2:4], 0)
    lines = jnp.concatenate(tiles[4:6], 0)
    for i in range(3):
        tap_grad[i] = lines[3 * i : 3 * i + 3]


def by_core(core, own, other):
    return jnp.where(core == 0, own, other), jnp.where(core == 0, other, own)


def state_kernel(where, proj, above, cot, wire, wire_pair, par, send1, send2, send3, signal, xs, gs, wires, halo):
    chunk = cot.shape[0]
    both = by_core(where[1], wire[...].astype(F32), wire_pair[...].astype(F32))
    wires[0:512, :] = jnp.stack(both, axis=1).reshape(512, LANES)
    early = lax.broadcasted_iota(jnp.int32, (8, LANES), 0) < 6

    for lane in range(8):
        parts = [rows_of_lines(wires[pl.ds(lane * 64 + q, 8, stride=8), :]) for q in range(8)]
        par[tile_rows(0, lane), :] = parts[4]
        par[tile_rows(1, lane), :] = parts[5]
        par[tile_rows(2, lane), :] = parts[0] + parts[2] + RATE_CENTRE
        par[tile_rows(3, lane), :] = parts[1] + jnp.where(early, parts[3], 0.0) + RATE_CENTRE
        par[tile_rows(4, lane), :] = parts[6] + parts[7]
        par[tile_rows(5, lane), :] = jnp.broadcast_to(parts[3][6:7] + parts[3][7:8], (8, LANES))

    @pl.loop(0, 8, unroll=2)
    def _(lane):
        weights = tap_weights(par, lane)
        for i in range(3):
            load_signal(i, proj, above, signal, lane)
        queries, keys, values = (taps(i, signal, weights, 0, chunk) for i in range(3))
        gated = rounded(keys * values)
        upstream = cot[:, column(lane)].astype(F32)
        gate_grad = rounded(upstream * queries)
        first = [signal[i, 8:16] for i in range(3)] + [upstream[0:8]]
        halo[pl.ds(pl.multiple_of(lane * 8, 8), 8), :] = head_rows(first)
        for tile in range(chunk // 8):
            xs[tile_rows(tile, lane), :] = gated[8 * tile : 8 * tile + 8]
            gs[tile_rows(tile, lane), :] = gate_grad[8 * tile : 8 * tile + 8]

    decay = decay_of(par)

    def step(tile, carry):
        forward, backward = map(list, carry)
        for i in range(8):
            x = xs[pl.ds(tile * 64 + i, 8, stride=8), :]
            g = gs[pl.ds((chunk // 8 - 1 - tile) * 64 + 7 - i, 8, stride=8), :]
            forward = [a * h + x for a, h in zip(decay, forward)]
            backward = [a * p + g for a, p in zip(decay, backward)]
        return tuple(forward), tuple(backward)

    zero = tuple(jnp.zeros((8, LANES), F32) for _ in range(ORDER))
    forward, backward = lax.fori_loop(0, chunk // 8, step, (zero, zero), unroll=2)
    send3[8 * ORDER :, :] = halo[...].astype(BF)
    for away, send in zip((1, 2, 3), (send1, send2, send3)):
        ahead = where[0] + away < 4
        for m in range(0, ORDER, 2):
            pair = [jnp.where(ahead, forward[n], backward[n]) for n in (m, m + 1)]
            send[8 * m : 8 * m + 16, :] = jnp.concatenate(pair, 0).astype(BF)


def final_kernel(*refs):
    (where, proj, above, cot, par, got1, got2, got3, *rest) = refs
    (out, proj_grad, sums_own, sums_pair, signal, tails, fgrads, xs, gs, ys, bs, queries_s, keys_s, values_s, held, sums, lines_s) = rest[-17:]
    chunk = cot.shape[0]
    tiles = chunk // 8
    follows = jnp.where(where[0] < 3, 1.0, 0.0)
    tails[...] = got3[8 * ORDER :, :].astype(F32) * follows

    @pl.loop(0, 8, unroll=2)
    def _(lane):
        weights = tap_weights(par, lane)
        for i in range(3):
            load_signal(i, proj, above, signal.at[lane], lane)
            signal[lane, i, 8 + chunk :] = padded(tails, lane, i)
        here = signal.at[lane]
        queries, keys, values = (taps(i, here, weights, 0, chunk + 8) for i in range(3))
        gated = rounded(keys * values)
        queries_s[lane] = queries
        keys_s[lane] = keys
        values_s[lane] = values
        for tile in range(tiles + 1):
            rows = slice(8 * tile, 8 * tile + 8)
            if tile < tiles:
                upstream = cot[rows, column(lane)].astype(F32)
            else:
                upstream = padded(tails, lane, 3)
            xs[tile_rows(tile, lane), :] = gated[rows]
            gs[tile_rows(tile, lane), :] = rounded(upstream * queries[rows])

    for group in range(0, ORDER, HALF):
        modes = range(group, group + HALF)
        rates = [jnp.exp(par[line_rows(ORDER + m), :]) for m in modes]
        decay = [jnp.exp(-r) for r in rates]
        gain = [par[line_rows(m), :] for m in modes]
        entering, leaving = [], []
        for n, m in enumerate(modes):
            whole = jnp.exp(-float(chunk) * rates[n])
            scales = [None, whole, whole * whole]
            enter, leave = jnp.zeros((8, LANES), F32), jnp.zeros((8, LANES), F32)
            for away, got in zip((1, 2, 3), (got1, got2, got3)):
                pair = got[16 * (m // 2) : 16 * (m // 2) + 16, :].astype(F32)
                state = pair[8 * (m % 2) : 8 * (m % 2) + 8]
                near = state if away == 1 else scales[away - 1] * state
                far = state if away == 3 else scales[3 - away] * state
                enter = enter + jnp.where(where[0] >= away, near, 0.0)
                leave = leave + jnp.where(where[0] < away, far, 0.0)
            entering.append(enter)
            leaving.append(leave)

        def store(ref, rows, value, group=group):
            if group:
                value = value + ref[rows, :]
            ref[rows, :] = value

        def forward(tile, carry):
            states, totals = map(list, carry)
            for i in range(8):
                rows = pl.ds(tile * 64 + i, 8, stride=8)
                x, g = xs[rows, :], gs[rows, :]
                for n in range(HALF):
                    held[tile * 8 + i, n] = states[n]
                states = [a * h + x for a, h in zip(decay, states)]
                totals = [t + g * h for t, h in zip(totals, states)]
                store(ys, rows, tree([r * h for r, h in zip(gain, states)]))
            return tuple(states), tuple(totals)

        zero = tuple(jnp.zeros((8, LANES), F32) for _ in modes)
        states, totals = lax.fori_loop(0, tiles, forward, (tuple(entering), zero), unroll=2)
        for i in range(2):
            rows = line_rows(chunk + i)
            states = [a * h + xs[rows, :] for a, h in zip(decay, states)]
            store(ys, rows, tree([r * h for r, h in zip(gain, states)]))

        def backward(step, carry):
            states, counts = map(list, carry)
            tile = tiles - 1 - step
            for i in range(7, -1, -1):
                rows = pl.ds(tile * 64 + i, 8, stride=8)
                g = gs[rows, :]
                states = [a * p + g for a, p in zip(decay, states)]
                counts = [c + p * held[tile * 8 + i, n] for n, (c, p) in enumerate(zip(counts, states))]
                store(bs, rows, tree([r * p for r, p in zip(gain, states)]))
            return tuple(states), tuple(counts)

        _, counts = lax.fori_loop(0, tiles, backward, (tuple(leaving), zero), unroll=2)
        store(bs, line_rows(chunk), tree([r * p for r, p in zip(gain, leaving)]))
        after = [(p - gs[line_rows(chunk), :]) / a for a, p in zip(decay, leaving)]
        store(bs, line_rows(chunk + 1), tree([r * p for r, p in zip(gain, after)]))
        for n, m in enumerate(modes):
            sums[line_rows(m), :] = totals[n]
            sums[line_rows(ORDER + m), :] = decay[n] * counts[n]

    two = lax.broadcasted_iota(jnp.int32, (8, LANES), 0) < 2

    @pl.loop(0, 8, unroll=2)
    def _(lane):
        weights = tap_weights(par, lane)
        upstream = cot[:, column(lane)].astype(F32)
        tail_up = padded(tails, lane, 3)
        convolved = rounded(jnp.concatenate([ys[tile_rows(t, lane), :] for t in range(tiles)], 0))
        gated_grad = rounded(jnp.concatenate([bs[tile_rows(t, lane), :] for t in range(tiles)], 0))
        tail_conv = rounded(jnp.where(two, ys[tile_rows(tiles, lane), :], 0.0))
        tail_back = rounded(jnp.where(two, bs[tile_rows(tiles, lane), :], 0.0))
        out[:, column(lane)] = (queries_s[lane, 0:chunk] * convolved).astype(BF)
        lines = []
        for i in range(3):
            if i == 0:
                grad, tail = upstream * convolved, tail_up * tail_conv
            else:
                other = values_s if i == 1 else keys_s
                grad = gated_grad * other[lane, 0:chunk]
                tail = tail_back * other[lane, chunk : chunk + 8]
            fgrads[i, 0:chunk] = grad
            fgrads[i, chunk:] = tail
            total = weights[3 * i] * grad
            for j in range(1, SHORT):
                total = total + weights[3 * i + j] * fgrads[i, j : j + chunk]
            proj_grad[i, :, column(lane)] = total.astype(BF)
            for j in range(SHORT):
                lines.append(jnp.sum(grad * signal[lane, i, 8 - j : 8 - j + chunk], axis=0, keepdims=True))
        sums[tile_rows(4, lane), :] = jnp.concatenate(lines[:8], 0)
        sums[tile_rows(5, lane), :] = jnp.concatenate([lines[8], jnp.zeros((7, LANES), F32)], 0)

    for lane in range(8):
        for q in range(SUM_ROWS // 8):
            lines_s[pl.ds(lane * 64 + q, 8, stride=8), :] = lines_of_rows(sums[tile_rows(q, lane), :])

    lines = lines_s[0:512, :].reshape(32, 2, 8, LANES)[:, :, : SUM_ROWS // 8].astype(BF)
    sums_own[...], sums_pair[...] = by_core(where[1], lines[:, 0], lines[:, 1])


def body(names, proj, short_weight, residue, log_decay, cotangent):
    ctx, devices, n_ctx = names
    chunk, channels = cotangent.shape[1:]
    own = residue.shape[1]
    seq = chunk * n_ctx
    n_dev = channels // own
    blocks = channels // WIDE
    runs = 2 if blocks % 2 == 0 else 1
    steps = blocks // runs
    zero = devices[1]
    n_zero = n_dev // n_ctx
    where = jnp.stack([lax.axis_index(ctx), lax.axis_index(zero) % 2]).astype(jnp.int32)
    cores = [[i for i in range(n_dev) if i % 2 == c] for c in range(2)]

    def from_all(values):
        return lax.all_to_all(values, devices, 0, 0, tiled=True, axis_index_groups=cores)

    def from_pair(values):
        return lax.ppermute(values, zero, [(i, i ^ 1) for i in range(n_zero)])


    spread = pl.pallas_call(
        spread_kernel,
        out_shape=jax.ShapeDtypeStruct((n_dev // 2, WIRE_ROWS // 8, 8 * own), BF),
        name="spread",
    )(short_weight, residue, log_decay)
    signal, spread = lax.optimization_barrier((proj[0].transpose(1, 0, 2), spread))
    wire = from_all(spread)

    upstream = cotangent[0]
    above = lax.ppermute(signal[:, chunk - 2 :], ctx, [(i, i + 1) for i in range(n_ctx - 1)])

    def shape(dims, kind):
        return jax.ShapeDtypeStruct(dims, kind)

    scalar = pl.BlockSpec(memory_space=pltpu.SMEM)
    anywhere = pl.BlockSpec(memory_space=pl.ANY)
    vmem = lambda *dims: pltpu.VMEM(dims, F32)
    params = pltpu.CompilerParams(vmem_limit_bytes=32 * 1024 * 1024)

    def specs(run):
        def wide(*dims):
            lead = len(dims)
            return pl.BlockSpec(dims + (WIDE,), lambda i: (0,) * lead + (i + run * steps,))

        def rows(count):
            return pl.BlockSpec((WIDE // own // 2, count // 8, 8 * own), lambda i: (i + run * steps, 0, 0))

        def whole(count):
            return pl.BlockSpec((None, count, LANES), lambda i: (i, 0, 0))

        def local(*dims):
            lead = len(dims)
            return pl.BlockSpec(dims + (WIDE,), lambda i: (0,) * lead + (i,))

        return wide, rows, whole, local

    width = steps * WIDE
    signals = [signal[:, :, run * width : run * width + width] for run in range(runs)]
    upstreams = [upstream[:, run * width : run * width + width] for run in range(runs)]

    wire, above, signals, upstreams = lax.optimization_barrier((wire, above, signals, upstreams))
    wire_pair = from_pair(wire)
    sizes = (8 * ORDER, 8 * ORDER, 8 * ORDER + 64)
    pars, gots = [], []
    for run in range(runs):
        wide, rows, whole, local = specs(run)
        par, *sent = pl.pallas_call(
            state_kernel,
            grid=(steps,),
            in_specs=[scalar, local(3, chunk), wide(3, 2), local(chunk), rows(WIRE_ROWS), rows(WIRE_ROWS)],
            out_specs=[whole(8 * PAR_ROWS)] + [whole(n) for n in sizes],
            out_shape=[shape((steps, 8 * PAR_ROWS, LANES), F32)]
            + [shape((steps, n, LANES), BF) for n in sizes],
            scratch_shapes=[
                vmem(3, chunk + 8, LANES), vmem(chunk * 8 + 8, LANES), vmem(chunk * 8 + 8, LANES), vmem(520, LANES),
                vmem(64, LANES),
            ],
            compiler_params=params,
            cost_estimate=pl.CostEstimate(flops=4 * 10**9, bytes_accessed=4 * 10**6, transcendentals=0),
            name="states",
        )(where, signals[run], above, upstreams[run], wire, wire_pair)
        pars.append(par)
        gots.append(
            [
                lax.ppermute(values, ctx, [(i, (i + k) % n_ctx) for i in range(n_ctx)])
                for k, values in zip((1, 2, 3), sent)
            ]
        )

    results = [
        shape((chunk, channels), BF),
        shape((3, chunk, channels), BF),
    ] + [shape((n_dev // 2, SUM_ROWS // 8, 8 * own), BF)] * 2
    made = []
    longer = chunk + 8
    for run in range(runs):
        wide, rows, whole, local = specs(run)
        made = pl.pallas_call(
            final_kernel,
            grid=(steps,),
            in_specs=[scalar, local(3, chunk), wide(3, 2), local(chunk), whole(8 * PAR_ROWS)]
            + [whole(n) for n in sizes]
            + [anywhere] * len(made),
            out_specs=[wide(chunk), wide(3, chunk), rows(SUM_ROWS), rows(SUM_ROWS)],
            out_shape=results,
            scratch_shapes=[
                vmem(8, 3, chunk + 16, LANES), vmem(64, LANES), vmem(3, longer, LANES),
                vmem(longer * 8 + 8, LANES), vmem(longer * 8 + 8, LANES),
                vmem(longer * 8 + 8, LANES), vmem(longer * 8 + 8, LANES),
                vmem(8, longer, LANES), vmem(8, longer, LANES), vmem(8, longer, LANES),
                vmem(chunk, HALF, 8, LANES), vmem(8 * SUM_ROWS, LANES), vmem(520, LANES),
            ],
            input_output_aliases={8 + i: i for i in range(len(made))},
            compiler_params=params,
            cost_estimate=pl.CostEstimate(flops=8 * 10**9, bytes_accessed=8 * 10**6, transcendentals=0),
            name="final",
        )(where, signals[run], above, upstreams[run], pars[run], *gots[run], *made)
    out, proj_grad, parts_own, parts_pair = made

    pair_sum = parts_own.astype(F32) + from_pair(parts_pair).astype(F32)
    arrived = from_all(pair_sum.astype(BF))
    tap_grad, residue_grad, decay_grad = pl.pallas_call(
        functools.partial(collect_kernel, 1.0 / seq),
        out_shape=[shape((3, SHORT, own), F32), shape((ORDER, own), F32), shape((ORDER, own), F32)],
        name="collect",
    )(arrived, residue, log_decay)
    return (
        out[None],
        proj_grad.transpose(1, 0, 2)[None],
        tap_grad,
        residue_grad,
        decay_grad,
    )


def solution(mesh):
    both = ("ctx", "zero")
    specs = (
        P("zero", "ctx", None, None),
        P(None, None, both),
        P(None, both),
        P(None, both),
        P("zero", "ctx", None),
    )
    out_specs = (specs[4], specs[0], specs[1], specs[2], specs[2])
    names = ("ctx", both, mesh.shape["ctx"])
    return jax.shard_map(
        functools.partial(body, names), mesh=mesh, in_specs=specs, out_specs=out_specs, check_vma=False
    )
```
